512 devices in a mesh: dp: 32 (over y, x, core), fsdp: 16 (over z).
Axes of the slice: x: 4, y: 4, z: 16, core: 2. Of those that a mesh axis runs over, the one named last changes fastest.
Arguments:
- activations: bfloat16 [24576, 8192], P('dp', 'fsdp'), may hold values from -6 to 6
- cotangent: bfloat16 [24576, 14336], P('dp', 'fsdp'), may hold values from -0.059814453 to 0.059814453
- basis: bfloat16 [8192, 1024], P('fsdp'), may hold values from -0.0625 to 0.0625
- first_moment: float32 [1024, 14336], P('dp', 'fsdp'), may hold values from -6 to 6
- second_moment: float32 [1024, 14336], P('dp', 'fsdp'), may hold values from 0.5 to 4
Outputs:
- moment_next: float32 [1024, 14336], P('dp', 'fsdp')
- square_next: float32 [1024, 14336], P('dp', 'fsdp')
- expanded: bfloat16 [8192, 14336], P('dp', 'fsdp')
The draws below stay inside these ranges and needn't reach their ends.
All inputs are finite; a program needn't handle non-finite values.
Results may differ from the reference program's by a relative error of at most 0.0035.
The reference program's roundings to bfloat16 on the way (of `projected` and `direction`) count: a program that leaves them out, or rounds other values in their place, can miss the bound.
Values may be sent and summed in bfloat16 or wider, within the bound.
No kernel may reach another device: no remote copies, remote signals or barrier semaphores. Data moves between devices by JAX's collectives and lax.ppermute only.
A program may use at most 64 MiB of HBM per device.

```python
import math
import jax
import jax.numpy as jnp
from jax import lax

D = 8192
F = 14336
R = 1024
TOKENS = 24576


def shard_levels(rng, shape, cuts, smallest, top_value):
    def one(axis_at, parts):
        steps = jax.random.uniform(jax.random.fold_in(jax.random.fold_in(rng, 6), axis_at), (parts,), jnp.float32, smallest / len(cuts), top_value / len(cuts))
        return jnp.repeat(jnp.exp(steps), shape[axis_at] // parts).reshape((-1,) + (1,) * (len(shape) - axis_at - 1))

    level = one(*cuts[0])
    for cut in cuts[1:]:
        level = level * one(*cut)
    return level


def scatter_about(stream_key, shape, width, reach, pieces=(), held_as=jnp.bfloat16):
    entries = jax.random.normal(stream_key, shape, jnp.float32) * width
    if len(pieces) > 0:
        entries = shard_levels(stream_key, shape, pieces, -0.22, 0.18) * entries
    return jnp.clip(entries, min=-reach, max=reach).astype(held_as)


def setup_inputs(seed: int = 0) -> dict:
    key_of = jax.random.split(jax.random.key(seed), 6)
    activations = scatter_about(key_of[0], (TOKENS, D), 1.0, 6.0, ((0, 32), (1, 16)))
    cotangent = scatter_about(key_of[1], (TOKENS, F), 0.01, 0.059814453, ((0, 32), (1, 16)))
    basis = scatter_about(key_of[2], (D, R), D ** -0.5, 0.0625, ((0, 16),))
    first_moment = scatter_about(key_of[3], (R, F), 1.0, 6.0, ((0, 32), (1, 16)), jnp.float32)
    second_moment = jnp.clip(jnp.exp(math.log(4.0) - 2.0794415 * jax.random.uniform(key_of[4], (R, F), jnp.float32) ** shard_levels(key_of[4], (R, F), ((0, 32), (1, 16)), -0.2, 0.2)), 0.5, 4.0)
    return {"activations": activations, "cotangent": cotangent, "basis": basis, "first_moment": first_moment, "second_moment": second_moment}


decay_first = 0.9
decay_second = 0.999
epsilon = 1e-08

def reference(activations, cotangent, basis, first_moment, second_moment):
    projected = jnp.dot(activations, basis, preferred_element_type=jnp.float32).astype(jnp.bfloat16)
    gradient = lax.dot_general(projected, cotangent, (((0,), (0,)), ((), ())), preferred_element_type=jnp.float32)
    moment_next = decay_first * first_moment + (1.0 - decay_first) * gradient
    square_next = decay_second * second_moment + (1.0 - decay_second) * gradient * gradient
    direction = (moment_next / (jnp.sqrt(square_next) + epsilon)).astype(jnp.bfloat16)
    expanded = jnp.dot(basis, direction, preferred_element_type=jnp.float32).astype(jnp.bfloat16)
    return (moment_next, square_next, expanded)
```

```python
import numpy as np
import jax
import jax.numpy as jnp
from jax import lax
from jax.experimental import pallas as pl
from jax.experimental.pallas import tpu as pltpu
from jax.sharding import Mesh, PartitionSpec as P

decay_first = 0.9
decay_second = 0.999
epsilon = 1e-08

SWAP = [(0, 1), (1, 0)]
VMEM_LIMIT = 40 * 1024 * 1024
LAST = (((1,), (1,)), ((), ()))
IN_VMEM = pl.BlockSpec(memory_space=pltpu.VMEM)
IN_HBM = pl.BlockSpec(memory_space=pl.ANY)
IN_SMEM = pl.BlockSpec(memory_space=pltpu.SMEM)


def params():
    return pltpu.CompilerParams(vmem_limit_bytes=VMEM_LIMIT)


def cost(flops, moved):
    return pl.CostEstimate(flops=flops, bytes_accessed=moved, transcendentals=0)


def project_own(own_rows, core_ref, basis_ref, act_ref, out_ref, picked_ref):
    rank = basis_ref.shape[1]
    at = lax.broadcasted_iota(jnp.int32, (rank // 2, rank), 0)
    wanted = at // own_rows * (2 * own_rows) + core_ref[0] * own_rows + at % own_rows
    pick = (lax.broadcasted_iota(jnp.int32, (rank // 2, rank), 1) == wanted).astype(jnp.bfloat16)
    picked = lax.dot_general(pick, basis_ref[...], LAST, preferred_element_type=jnp.float32).astype(jnp.bfloat16)
    picked_ref[...] = picked
    out_ref[...] = lax.dot_general(picked, act_ref[...], LAST, preferred_element_type=jnp.float32)[None]


def project_other(picked_ref, act_ref, _, out_ref):
    out_ref[...] = lax.dot_general(picked_ref[...], act_ref[...], LAST, preferred_element_type=jnp.float32)[None]


def grad_terms(proj_ref, own_ref, other_ref, _, out_ref):
    total = jnp.dot(proj_ref[0], own_ref[...], preferred_element_type=jnp.float32)
    total += jnp.dot(proj_ref[1], other_ref[...], preferred_element_type=jnp.float32)
    out_ref[...] = total.astype(jnp.bfloat16)


def adam(terms_ref, first_ref, second_ref, moment_ref, square_ref, copies_ref):
    gradient = terms_ref[0].astype(jnp.float32)
    for i in range(1, terms_ref.shape[0]):
        gradient += terms_ref[i].astype(jnp.float32)
    moment_next = decay_first * first_ref[...] + (1.0 - decay_first) * gradient
    square_next = decay_second * second_ref[...] + (1.0 - decay_second) * gradient * gradient
    moment_ref[...] = moment_next
    square_ref[...] = square_next
    direction = (moment_next / (jnp.sqrt(square_next) + epsilon)).astype(jnp.bfloat16)
    for i in range(copies_ref.shape[0]):
        copies_ref[i] = direction


def expand(core_ref, shard_ref, mine_ref, other_ref, out_ref, all_ref):
    block_rows = out_ref.shape[0]
    core = core_ref[0]
    all_ref[:, pl.ds(core, 1)] = mine_ref[...][:, None]
    all_ref[:, pl.ds(1 - core, 1)] = other_ref[...][:, None]
    rows = pl.ds(pl.multiple_of(core * block_rows, block_rows), block_rows)
    direction = all_ref[...].reshape(shard_ref.shape[1], out_ref.shape[1])
    out_ref[...] = jnp.dot(shard_ref[rows, :], direction, preferred_element_type=jnp.float32).astype(jnp.bfloat16)


def body(activations, cotangent, basis, first_moment, second_moment):
    chips = lax.axis_size("chip")
    shards = lax.axis_size("fsdp")
    features, rank = basis.shape
    tokens = activations.shape[0]
    own_rows, columns = first_moment.shape
    chip, core, shard = lax.axis_index("chip"), lax.axis_index("core"), lax.axis_index("fsdp")
    core_at = core.astype(jnp.int32).reshape(1)
    f32, bf16 = jnp.float32, jnp.bfloat16

    piece_rows = features // shards
    piece = lax.dynamic_slice_in_dim(basis, (chip + shards - shard) % shards * piece_rows, piece_rows, 0)
    hand_on = [
        ((p * 2 + c) * shards + k, (k * 2 + c) * shards + (p - k) % shards)
        for p in range(chips) for c in range(2) for k in range(shards)
    ]
    piece = lax.ppermute(piece, ("chip", "core", "fsdp"), hand_on)
    chip_basis = lax.all_gather(piece, "fsdp", axis=0, tiled=True)

    other_act = lax.ppermute(activations, "core", SWAP)
    other_cot = lax.ppermute(cotangent, "core", SWAP)
    flops = rank * tokens * features
    partial, picked = pl.pallas_call(
        lambda *refs: project_own(own_rows, *refs),
        grid=(1,),
        out_shape=(
            jax.ShapeDtypeStruct((2, rank // 2, tokens), f32),
            jax.ShapeDtypeStruct((rank // 2, features), bf16),
        ),
        in_specs=[IN_SMEM, pl.BlockSpec((features, rank), lambda i: (0, 0)), pl.BlockSpec((tokens, features), lambda i: (0, 0))],
        out_specs=(
            pl.BlockSpec((1, rank // 2, tokens), lambda i: (0, 0, 0)),
            pl.BlockSpec((rank // 2, features), lambda i: (0, 0)),
        ),
        compiler_params=params(),
        cost_estimate=cost(flops * 2, 5 << 20),
    )(core_at, basis, activations)
    partial = pl.pallas_call(
        project_other,
        grid=(1,),
        out_shape=jax.ShapeDtypeStruct((2, rank // 2, tokens), f32),
        in_specs=[
            pl.BlockSpec((rank // 2, features), lambda i: (0, 0)),
            pl.BlockSpec((tokens, features), lambda i: (0, 0)),
            IN_HBM,
        ],
        out_specs=pl.BlockSpec((1, rank // 2, tokens), lambda i: (1, 0, 0)),
        input_output_aliases={2: 0},
        compiler_params=params(),
        cost_estimate=cost(flops, 3 << 20),
    )(picked, other_act, partial)
    projected = lax.psum(partial, "fsdp").astype(bf16)

    terms = pl.pallas_call(
        grad_terms,
        out_shape=jax.ShapeDtypeStruct((rank // 2, columns), bf16),
        in_specs=[IN_VMEM, IN_VMEM, IN_VMEM, IN_HBM],
        out_specs=IN_VMEM,
        compiler_params=params(),
        cost_estimate=cost(2 * rank * tokens * columns, 5 << 20),
    )(projected, cotangent, other_cot, chip_basis)
    terms = lax.all_to_all(terms.reshape(chips, own_rows, columns), "chip", 0, 0, tiled=True)

    moment_next, square_next, copies = pl.pallas_call(
        adam,
        out_shape=(
            jax.ShapeDtypeStruct((own_rows, columns), f32),
            jax.ShapeDtypeStruct((own_rows, columns), f32),
            jax.ShapeDtypeStruct((chips, own_rows, columns), bf16),
        ),
        in_specs=[IN_VMEM] * 3,
        out_specs=(IN_VMEM,) * 3,
        compiler_params=params(),
        cost_estimate=cost(1 << 20, 2 << 20),
    )(terms, first_moment, second_moment)
    mine = lax.all_to_all(copies, "chip", 0, 0, tiled=True)
    other = lax.ppermute(mine, "core", SWAP)
    expanded = pl.pallas_call(
        expand,
        out_shape=jax.ShapeDtypeStruct((features // 2, columns), bf16),
        in_specs=[IN_SMEM] + [IN_VMEM] * 3,
        out_specs=IN_VMEM,
        scratch_shapes=[pltpu.VMEM((chips, 2, own_rows, columns), bf16)],
        compiler_params=params(),
        cost_estimate=cost(features * rank * columns, 4 << 20),
    )(core_at, chip_basis, mine, other)
    return (moment_next, square_next, expanded)


def solution(mesh):
    devices = np.asarray(mesh.devices)
    inner = Mesh(devices.reshape(devices.shape[0] // 2, 2, devices.shape[1]), ("chip", "core", "fsdp"))
    split = P(("chip", "core"), "fsdp")
    in_specs = (split, split, P("fsdp", None), split, split)
    return jax.shard_map(body, mesh=inner, in_specs=in_specs, out_specs=(split, split, split), check_vma=False)
```

```python
import numpy as np
import jax
import jax.numpy as jnp
from jax import lax
from jax.experimental import pallas as pl
from jax.experimental.pallas import tpu as pltpu
from jax.sharding import Mesh, PartitionSpec as P

decay_first = 0.9
decay_second = 0.999
epsilon = 1e-08

SWAP = [(0, 1), (1, 0)]
VMEM_LIMIT = 40 * 1024 * 1024
LAST = (((1,), (1,)), ((), ()))
IN_VMEM = pl.BlockSpec(memory_space=pltpu.VMEM)
IN_HBM = pl.BlockSpec(memory_space=pltpu.HBM)
IN_SMEM = pl.BlockSpec(memory_space=pltpu.SMEM)


def params(limit=VMEM_LIMIT):
    return pltpu.CompilerParams(vmem_limit_bytes=limit)


def cost(flops, moved):
    return pl.CostEstimate(flops=flops, bytes_accessed=moved, transcendentals=0)


def project_own(own_rows, place_ref, basis_hbm, act_hbm, out_hbm, picked_ref, basis_ref, act_ref, own_ref, block_ref, sems):
    features, rank = basis_ref.shape
    tokens = act_ref.shape[0]
    half = rank // 2
    rows = features // 2
    core, holds = place_ref[0], place_ref[1]
    load_basis = pltpu.make_async_copy(basis_hbm, basis_ref, sems.at[0])
    load_act = pltpu.make_async_copy(act_hbm, act_ref, sems.at[1])
    load_basis.start()
    load_act.start()
    at = lax.broadcasted_iota(jnp.int32, (half, rank), 0)
    wanted = at // own_rows * (2 * own_rows) + core * own_rows + at % own_rows
    pick = (lax.broadcasted_iota(jnp.int32, (half, rank), 1) == wanted).astype(jnp.bfloat16)
    load_basis.wait()
    mine = basis_ref[pl.ds(pl.multiple_of(core * rows, rows), rows), :].astype(jnp.float32)
    mine = jnp.where(holds == 1, mine, 0.0)
    block_ref[:rows, :] = mine[:, :half]
    block_ref[rows:, :] = mine[:, half:]
    save_block = pltpu.make_async_copy(block_ref, out_hbm.at[:, pl.ds(2 * tokens, half)], sems.at[2])
    save_block.start()
    picked = lax.dot_general(pick, basis_ref[...], LAST, preferred_element_type=jnp.float32).astype(jnp.bfloat16)
    picked_ref[...] = picked
    load_act.wait()
    own_ref[...] = lax.dot_general(picked, act_ref[...], LAST, preferred_element_type=jnp.float32)
    save_own = pltpu.make_async_copy(own_ref, out_hbm.at[:, pl.ds(0, tokens)], sems.at[3])
    save_own.start()
    save_block.wait()
    save_own.wait()


def project_other(picked_ref, act_ref, _, out_hbm, other_ref, sems):
    tokens = act_ref.shape[0]
    half = other_ref.shape[0] // 2
    copies = []
    for i in range(2):
        rows = pl.ds(i * half, half)
        other_ref[rows, :] = lax.dot_general(picked_ref[rows, :], act_ref[...], LAST, preferred_element_type=jnp.float32)
        copies.append(pltpu.make_async_copy(other_ref.at[rows, :], out_hbm.at[rows, pl.ds(tokens, tokens)], sems.at[i]))
        copies[i].start()
    for copy in copies:
        copy.wait()


def grad_terms(proj_ref, own_ref, other_hbm, out_ref, other_ref, sems):
    tokens = own_ref.shape[0]
    part = tokens // 4
    copies = []
    for i in range(4):
        rows = pl.ds(i * part, part)
        copies.append(pltpu.make_async_copy(other_hbm.at[rows, :], other_ref.at[rows, :], sems.at[i]))
        copies[i].start()
    total = jnp.dot(proj_ref[:, :tokens], own_ref[...], preferred_element_type=jnp.float32)
    for copy in copies:
        copy.wait()
    total += jnp.dot(proj_ref[:, tokens : 2 * tokens], other_ref[...], preferred_element_type=jnp.float32)
    out_ref[...] = total.astype(jnp.bfloat16)


def adam(terms_ref, first_ref, second_ref, moment_ref, square_ref, copies_ref):
    gradient = terms_ref[0].astype(jnp.float32)
    for i in range(1, terms_ref.shape[0]):
        gradient += terms_ref[i].astype(jnp.float32)
    moment_next = decay_first * first_ref[...] + (1.0 - decay_first) * gradient
    square_next = decay_second * second_ref[...] + (1.0 - decay_second) * gradient * gradient
    moment_ref[...] = moment_next
    square_ref[...] = square_next
    direction = (moment_next / (jnp.sqrt(square_next) + epsilon)).astype(jnp.bfloat16)
    for i in range(copies_ref.shape[0]):
        copies_ref[i] = direction


def expand(place_ref, summed_hbm, mine_ref, other_ref, out_ref, block_ref, all_ref, sem):
    half = block_ref.shape[0]
    columns = out_ref.shape[1]
    rows = out_ref.shape[0]
    core = place_ref[0]
    copy = pltpu.make_async_copy(summed_hbm.at[:, pl.ds(summed_hbm.shape[1] - half, half)], block_ref, sem)
    copy.start()
    all_ref[:, pl.ds(core, 1)] = mine_ref[...][:, None]
    all_ref[:, pl.ds(1 - core, 1)] = other_ref[...][:, None]
    direction = all_ref[...].reshape(2 * half, columns)
    copy.wait()
    total = jnp.dot(block_ref[:rows, :], direction[:half], preferred_element_type=jnp.float32)
    total += jnp.dot(block_ref[rows:, :], direction[half:], preferred_element_type=jnp.float32)
    out_ref[...] = total.astype(jnp.bfloat16)


def body(activations, cotangent, basis, first_moment, second_moment):
    chips = lax.axis_size("chip")
    features, rank = basis.shape
    tokens = activations.shape[0]
    half = rank // 2
    own_rows, columns = first_moment.shape
    core = lax.axis_index("core")
    holds = lax.axis_index("chip") == lax.axis_index("fsdp")
    place = jnp.stack([core, holds]).astype(jnp.int32)
    f32, bf16 = jnp.float32, jnp.bfloat16

    other_act = lax.ppermute(activations, "core", SWAP)
    other_cot = lax.ppermute(cotangent, "core", SWAP)
    partial, picked = pl.pallas_call(
        lambda *refs: project_own(own_rows, *refs),
        out_shape=(pltpu.HBM((half, 2 * tokens + half), f32), pltpu.VMEM((half, features), bf16)),
        in_specs=[IN_SMEM, IN_HBM, IN_HBM],
        out_specs=(IN_HBM, IN_VMEM),
        scratch_shapes=[
            pltpu.VMEM((features, rank), bf16),
            pltpu.VMEM((tokens, features), bf16),
            pltpu.VMEM((half, tokens), f32),
            pltpu.VMEM((half, half), f32),
            pltpu.SemaphoreType.DMA((4,)),
        ],
        compiler_params=params(60 * 1024 * 1024),
        cost_estimate=cost(2 * rank * tokens * features, 5 << 20),
    )(place, basis, activations)
    partial = pl.pallas_call(
        project_other,
        out_shape=pltpu.HBM((half, 2 * tokens + half), f32),
        in_specs=[IN_VMEM, IN_VMEM, IN_HBM],
        out_specs=IN_HBM,
        scratch_shapes=[pltpu.VMEM((half, tokens), f32), pltpu.SemaphoreType.DMA((2,))],
        input_output_aliases={2: 0},
        compiler_params=params(),
        cost_estimate=cost(rank * tokens * features, 3 << 20),
    )(picked, other_act, partial)
    summed = lax.psum(partial, "fsdp").astype(bf16)

    terms = pl.pallas_call(
        grad_terms,
        out_shape=jax.ShapeDtypeStruct((half, columns), bf16),
        in_specs=[IN_VMEM, IN_VMEM, IN_HBM],
        out_specs=IN_VMEM,
        scratch_shapes=[pltpu.VMEM((tokens, columns), bf16), pltpu.SemaphoreType.DMA((4,))],
        compiler_params=params(),
        cost_estimate=cost(2 * rank * tokens * columns, 5 << 20),
    )(summed, cotangent, other_cot)
    terms = lax.all_to_all(terms.reshape(chips, own_rows, columns), "chip", 0, 0, tiled=True)

    moment_next, square_next, copies = pl.pallas_call(
        adam,
        out_shape=(
            jax.ShapeDtypeStruct((own_rows, columns), f32),
            jax.ShapeDtypeStruct((own_rows, columns), f32),
            jax.ShapeDtypeStruct((chips, own_rows, columns), bf16),
        ),
        in_specs=[IN_VMEM] * 3,
        out_specs=(IN_VMEM,) * 3,
        compiler_params=params(),
        cost_estimate=cost(1 << 20, 2 << 20),
    )(terms, first_moment, second_moment)
    mine = lax.all_to_all(copies, "chip", 0, 0, tiled=True)
    other = lax.ppermute(mine, "core", SWAP)
    expanded = pl.pallas_call(
        expand,
        out_shape=jax.ShapeDtypeStruct((features // 2, columns), bf16),
        in_specs=[IN_SMEM, IN_HBM, IN_VMEM, IN_VMEM],
        out_specs=IN_VMEM,
        scratch_shapes=[
            pltpu.VMEM((half, half), bf16),
            pltpu.VMEM((chips, 2, own_rows, columns), bf16),
            pltpu.SemaphoreType.DMA,
        ],
        compiler_params=params(),
        cost_estimate=cost(features * rank * columns, 4 << 20),
    )(place, summed, mine, other)
    return (moment_next, square_next, expanded)


def solution(mesh):
    devices = np.asarray(mesh.devices)
    inner = Mesh(devices.reshape(devices.shape[0] // 2, 2, devices.shape[1]), ("chip", "core", "fsdp"))
    split = P(("chip", "core"), "fsdp")
    in_specs = (split, split, P("fsdp", None), split, split)
    return jax.shard_map(body, mesh=inner, in_specs=in_specs, out_specs=(split, split, split), check_vma=False)
```

```python
import numpy as np
import jax
import jax.numpy as jnp
from jax import lax
from jax.experimental import pallas as pl
from jax.experimental.pallas import tpu as pltpu
from jax.sharding import Mesh, PartitionSpec as P

decay_first = 0.9
decay_second = 0.999
epsilon = 1e-08

SWAP = [(0, 1), (1, 0)]
VMEM_LIMIT = 40 * 1024 * 1024
LAST = (((1,), (1,)), ((), ()))
IN_VMEM = pl.BlockSpec(memory_space=pltpu.VMEM)
IN_HBM = pl.BlockSpec(memory_space=pltpu.HBM)
IN_SMEM = pl.BlockSpec(memory_space=pltpu.SMEM)


def params(limit=VMEM_LIMIT):
    return pltpu.CompilerParams(vmem_limit_bytes=limit)


def cost(flops, moved):
    return pl.CostEstimate(flops=flops, bytes_accessed=moved, transcendentals=0)


def project_rows(picked_ref, act_ref, out_ref, out_hbm, sems):
    part = out_ref.shape[0] // 4
    copies = []
    for i in range(4):
        rows = pl.ds(i * part, part)
        out_ref[rows, :] = lax.dot_general(picked_ref[rows, :], act_ref[...], LAST, preferred_element_type=jnp.float32)
        copies.append(pltpu.make_async_copy(out_ref.at[rows, :], out_hbm.at[rows, :], sems.at[i]))
        copies[i].start()
    for copy in copies:
        copy.wait()


def project_own(own_rows, place_ref, basis_hbm, act_hbm, out_hbm, picked_ref, basis_ref, act_ref, out_ref, sems):
    features, rank = basis_ref.shape
    half = rank // 2
    copies = []
    for hbm, ref in ((basis_hbm, basis_ref), (act_hbm, act_ref)):
        part = ref.shape[0] // 4
        for i in range(4):
            rows = pl.ds(i * part, part)
            copies.append(pltpu.make_async_copy(hbm.at[rows, :], ref.at[rows, :], sems.at[len(copies)]))
            copies[-1].start()
    at = lax.broadcasted_iota(jnp.int32, (half, rank), 0)
    wanted = at // own_rows * (2 * own_rows) + place_ref[0] * own_rows + at % own_rows
    pick = (lax.broadcasted_iota(jnp.int32, (half, rank), 1) == wanted).astype(jnp.bfloat16)
    for copy in copies[:4]:
        copy.wait()
    picked = lax.dot_general(pick, basis_ref[...], LAST, preferred_element_type=jnp.float32).astype(jnp.bfloat16)
    picked_ref[...] = picked
    for copy in copies[4:]:
        copy.wait()
    project_rows(picked_ref, act_ref, out_ref, out_hbm.at[0], sems)


def project_other(picked_ref, act_ref, _, out_hbm, out_ref, sems):
    project_rows(picked_ref, act_ref, out_ref, out_hbm.at[1], sems)


def grad_terms(proj_ref, own_ref, other_hbm, _, out_ref, other_ref, sems):
    tokens = own_ref.shape[0]
    part = tokens // 4
    copies = []
    for i in range(4):
        rows = pl.ds(i * part, part)
        copies.append(pltpu.make_async_copy(other_hbm.at[rows, :], other_ref.at[rows, :], sems.at[i]))
        copies[i].start()
    total = jnp.dot(proj_ref[0], own_ref[...], preferred_element_type=jnp.float32)
    for copy in copies:
        copy.wait()
    total += jnp.dot(proj_ref[1], other_ref[...], preferred_element_type=jnp.float32)
    out_ref[...] = total.astype(jnp.bfloat16)


def adam(terms_ref, first_ref, second_ref, moment_ref, square_ref, copies_ref):
    gradient = terms_ref[0].astype(jnp.float32)
    for i in range(1, terms_ref.shape[0]):
        gradient += terms_ref[i].astype(jnp.float32)
    moment_next = decay_first * first_ref[...] + (1.0 - decay_first) * gradient
    square_next = decay_second * second_ref[...] + (1.0 - decay_second) * gradient * gradient
    moment_ref[...] = moment_next
    square_ref[...] = square_next
    direction = (moment_next / (jnp.sqrt(square_next) + epsilon)).astype(jnp.bfloat16)
    for i in range(copies_ref.shape[0]):
        copies_ref[i] = direction


def expand(place_ref, block_hbm, mine_ref, other_ref, out_ref, block_ref, all_ref, sem):
    core = place_ref[0]
    copy = pltpu.make_async_copy(block_hbm, block_ref, sem)
    copy.start()
    all_ref[:, pl.ds(core, 1)] = mine_ref[...][:, None]
    all_ref[:, pl.ds(1 - core, 1)] = other_ref[...][:, None]
    direction = all_ref[...].reshape(block_ref.shape[1], out_ref.shape[1])
    copy.wait()
    out_ref[...] = jnp.dot(block_ref[...], direction, preferred_element_type=jnp.float32).astype(jnp.bfloat16)


def block_pairs(chips):
    pairs = []
    for p in range(chips):
        for k in range(chips):
            z = (k + p // 4 + 4 * ((p + k) % 4)) % chips
            pairs += [((p * 2 + c) * chips + k, (k * 2 + c) * chips + z) for c in range(2)]
    return pairs


def body(activations, cotangent, basis, first_moment, second_moment):
    chips = lax.axis_size("chip")
    features, rank = basis.shape
    tokens = activations.shape[0]
    half = rank // 2
    own_rows, columns = first_moment.shape
    core = lax.axis_index("core")
    place = core.astype(jnp.int32).reshape(1)
    f32, bf16 = jnp.float32, jnp.bfloat16

    rows = features // 2
    block = lax.dynamic_slice_in_dim(basis, core * rows, rows, 0)
    block = lax.ppermute(block, ("chip", "core", "fsdp"), block_pairs(chips))

    other_act = lax.ppermute(activations, "core", SWAP)
    other_cot = lax.ppermute(cotangent, "core", SWAP)
    partial, picked = pl.pallas_call(
        lambda *refs: project_own(own_rows, *refs),
        out_shape=(pltpu.HBM((2, half, tokens), f32), pltpu.VMEM((half, features), bf16)),
        in_specs=[IN_SMEM, IN_HBM, IN_HBM],
        out_specs=(IN_HBM, IN_VMEM),
        scratch_shapes=[
            pltpu.VMEM((features, rank), bf16),
            pltpu.VMEM((tokens, features), bf16),
            pltpu.VMEM((half, tokens), f32),
            pltpu.SemaphoreType.DMA((8,)),
        ],
        compiler_params=params(55 * 1024 * 1024),
        cost_estimate=cost(2 * rank * tokens * features, 5 << 20),
    )(place, basis, activations)
    partial = pl.pallas_call(
        project_other,
        out_shape=pltpu.HBM((2, half, tokens), f32),
        in_specs=[IN_VMEM, IN_VMEM, IN_HBM],
        out_specs=IN_HBM,
        scratch_shapes=[pltpu.VMEM((half, tokens), f32), pltpu.SemaphoreType.DMA((4,))],
        input_output_aliases={2: 0},
        compiler_params=params(),
        cost_estimate=cost(rank * tokens * features, 3 << 20),
    )(picked, other_act, partial)
    projected = lax.psum(partial, "fsdp").astype(bf16)

    terms = pl.pallas_call(
        grad_terms,
        out_shape=jax.ShapeDtypeStruct((half, columns), bf16),
        in_specs=[IN_VMEM, IN_VMEM, IN_HBM, IN_HBM],
        out_specs=IN_VMEM,
        scratch_shapes=[pltpu.VMEM((tokens, columns), bf16), pltpu.SemaphoreType.DMA((4,))],
        compiler_params=params(),
        cost_estimate=cost(2 * rank * tokens * columns, 5 << 20),
    )(projected, cotangent, other_cot, block)
    terms = lax.all_to_all(terms.reshape(chips, own_rows, columns), "chip", 0, 0, tiled=True)

    moment_next, square_next, copies = pl.pallas_call(
        adam,
        out_shape=(
            jax.ShapeDtypeStruct((own_rows, columns), f32),
            jax.ShapeDtypeStruct((own_rows, columns), f32),
            jax.ShapeDtypeStruct((chips, own_rows, columns), bf16),
        ),
        in_specs=[IN_VMEM] * 3,
        out_specs=(IN_VMEM,) * 3,
        compiler_params=params(),
        cost_estimate=cost(1 << 20, 2 << 20),
    )(terms, first_moment, second_moment)
    mine = lax.all_to_all(copies, "chip", 0, 0, tiled=True)
    other = lax.ppermute(mine, "core", SWAP)
    expanded = pl.pallas_call(
        expand,
        out_shape=jax.ShapeDtypeStruct((features // 2, columns), bf16),
        in_specs=[IN_SMEM, IN_HBM, IN_VMEM, IN_VMEM],
        out_specs=IN_VMEM,
        scratch_shapes=[
            pltpu.VMEM((rows, rank), bf16),
            pltpu.VMEM((chips, 2, own_rows, columns), bf16),
            pltpu.SemaphoreType.DMA,
        ],
        compiler_params=params(),
        cost_estimate=cost(features * rank * columns, 4 << 20),
    )(place, block, mine, other)
    return (moment_next, square_next, expanded)


def solution(mesh):
    devices = np.asarray(mesh.devices)
    inner = Mesh(devices.reshape(devices.shape[0] // 2, 2, devices.shape[1]), ("chip", "core", "fsdp"))
    split = P(("chip", "core"), "fsdp")
    in_specs = (split, split, P("fsdp", None), split, split)
    return jax.shard_map(body, mesh=inner, in_specs=in_specs, out_specs=(split, split, split), check_vma=False)
```

```python
import numpy as np
import jax
import jax.numpy as jnp
from jax import lax
from jax.experimental import pallas as pl
from jax.experimental.pallas import tpu as pltpu
from jax.sharding import Mesh, PartitionSpec as P

decay_first = 0.9
decay_second = 0.999
epsilon = 1e-08

SWAP = [(0, 1), (1, 0)]
VMEM_LIMIT = 40 * 1024 * 1024
LAST = (((1,), (1,)), ((), ()))
IN_VMEM = pl.BlockSpec(memory_space=pltpu.VMEM)
IN_HBM = pl.BlockSpec(memory_space=pltpu.HBM)
IN_SMEM = pl.BlockSpec(memory_space=pltpu.SMEM)


def params(limit=VMEM_LIMIT):
    return pltpu.CompilerParams(vmem_limit_bytes=limit)


def cost(flops, moved):
    return pl.CostEstimate(flops=flops, bytes_accessed=moved, transcendentals=0)


def project(own_rows, core_ref, holds_ref, basis_hbm, own_hbm, other_hbm, out_hbm, basis_ref, own_ref, other_ref, out_ref, sems):
    features, rank = basis_ref.shape
    tokens = own_ref.shape[0]
    half = rank // 2
    rows = features // 2
    load_basis = pltpu.make_async_copy(basis_hbm, basis_ref, sems.at[0])
    load_own = pltpu.make_async_copy(own_hbm, own_ref, sems.at[1])
    load_basis.start()
    load_own.start()
    load_other = pltpu.make_async_copy(other_hbm, other_ref, sems.at[2])
    load_other.start()
    at = lax.broadcasted_iota(jnp.int32, (half, rank), 0)
    wanted = at // own_rows * (2 * own_rows) + core_ref[0] * own_rows + at % own_rows
    pick = (lax.broadcasted_iota(jnp.int32, (half, rank), 1) == wanted).astype(jnp.bfloat16)
    load_basis.wait()
    picked = lax.dot_general(pick, basis_ref[...], LAST, preferred_element_type=jnp.float32).astype(jnp.bfloat16)
    saves = []

    def save(start, size):
        here = pl.ds(start, size)
        saves.append(pltpu.make_async_copy(out_ref.at[:, here], out_hbm.at[:, here], sems.at[3 + len(saves)]))
        saves[-1].start()

    load_own.wait()
    out_ref[:, :tokens] = lax.dot_general(picked, own_ref[...], LAST, preferred_element_type=jnp.float32)
    save(0, tokens)
    load_other.wait()
    out_ref[:, tokens : 2 * tokens] = lax.dot_general(picked, other_ref[...], LAST, preferred_element_type=jnp.float32)
    save(tokens, tokens)
    mine = basis_ref[pl.ds(pl.multiple_of(core_ref[0] * rows, rows), rows), :].astype(jnp.float32)
    mine = jnp.where(holds_ref[0] == 1, mine, 0.0)
    out_ref[:rows, 2 * tokens :] = mine[:, :half]
    out_ref[rows:, 2 * tokens :] = mine[:, half:]
    save(2 * tokens, half)
    for copy in saves:
        copy.wait()


def grad_terms(summed_ref, own_ref, other_hbm, out_ref, other_ref, sems):
    tokens = own_ref.shape[0]
    first = tokens // 3 * 2
    copies = []
    for i, (start, size) in enumerate(((0, first), (first, tokens - first))):
        rows = pl.ds(start, size)
        copies.append(pltpu.make_async_copy(other_hbm.at[rows, :], other_ref.at[rows, :], sems.at[i]))
        copies[i].start()
    total = jnp.dot(summed_ref[:, :tokens], own_ref[...], preferred_element_type=jnp.float32)
    copies[0].wait()
    total += jnp.dot(summed_ref[:, tokens : tokens + first], other_ref[:first, :], preferred_element_type=jnp.float32)
    copies[1].wait()
    total += jnp.dot(summed_ref[:, tokens + first : 2 * tokens], other_ref[first:, :], preferred_element_type=jnp.float32)
    out_ref[...] = total.astype(jnp.bfloat16)


def adam(terms_ref, first_ref, second_ref, moment_ref, square_ref, copies_ref):
    gradient = terms_ref[0].astype(jnp.float32)
    for i in range(1, terms_ref.shape[0]):
        gradient += terms_ref[i].astype(jnp.float32)
    moment_next = decay_first * first_ref[...] + (1.0 - decay_first) * gradient
    square_next = decay_second * second_ref[...] + (1.0 - decay_second) * gradient * gradient
    moment_ref[...] = moment_next
    square_ref[...] = square_next
    direction = (moment_next / (jnp.sqrt(square_next) + epsilon)).astype(jnp.bfloat16)
    for i in range(copies_ref.shape[0]):
        copies_ref[i] = direction


def expand(core_ref, summed_ref, mine_ref, other_ref, out_ref, all_ref):
    rows, columns = out_ref.shape
    half = summed_ref.shape[0]
    start = summed_ref.shape[1] - half
    core = core_ref[0]
    all_ref[:, pl.ds(core, 1)] = mine_ref[...][:, None]
    all_ref[:, pl.ds(1 - core, 1)] = other_ref[...][:, None]
    direction = all_ref[...].reshape(2 * half, columns)
    total = jnp.dot(summed_ref[:rows, start:], direction[:half], preferred_element_type=jnp.float32)
    total += jnp.dot(summed_ref[rows:, start:], direction[half:], preferred_element_type=jnp.float32)
    out_ref[...] = total.astype(jnp.bfloat16)


def body(activations, cotangent, basis, first_moment, second_moment):
    chips = lax.axis_size("chip")
    features, rank = basis.shape
    tokens = activations.shape[0]
    half = rank // 2
    own_rows, columns = first_moment.shape
    core = lax.axis_index("core").astype(jnp.int32).reshape(1)
    holds = (lax.axis_index("chip") == lax.axis_index("fsdp")).astype(jnp.int32).reshape(1)
    f32, bf16 = jnp.float32, jnp.bfloat16

    other_act = lax.ppermute(activations, "core", SWAP)
    other_cot = lax.ppermute(cotangent, "core", SWAP)
    partial = pl.pallas_call(
        lambda *refs: project(own_rows, *refs),
        out_shape=pltpu.HBM((half, 2 * tokens + half), f32),
        in_specs=[IN_SMEM, IN_SMEM, IN_HBM, IN_HBM, IN_HBM],
        out_specs=IN_HBM,
        scratch_shapes=[
            pltpu.VMEM((features, rank), bf16),
            pltpu.VMEM((tokens, features), bf16),
            pltpu.VMEM((tokens, features), bf16),
            pltpu.VMEM((half, 2 * tokens + half), f32),
            pltpu.SemaphoreType.DMA((6,)),
        ],
        compiler_params=params(55 * 1024 * 1024),
        cost_estimate=cost(3 * rank * tokens * features, 7 << 20),
    )(core, holds, basis, activations, other_act)
    summed = lax.psum(partial, "fsdp").astype(bf16)

    terms = pl.pallas_call(
        grad_terms,
        out_shape=jax.ShapeDtypeStruct((half, columns), bf16),
        in_specs=[IN_VMEM, IN_VMEM, IN_HBM],
        out_specs=IN_VMEM,
        scratch_shapes=[pltpu.VMEM((tokens, columns), bf16), pltpu.SemaphoreType.DMA((2,))],
        compiler_params=params(),
        cost_estimate=cost(2 * rank * tokens * columns, 5 << 20),
    )(summed, cotangent, other_cot)
    terms = lax.all_to_all(terms.reshape(chips, own_rows, columns), "chip", 0, 0, tiled=True)

    moment_next, square_next, copies = pl.pallas_call(
        adam,
        out_shape=(
            jax.ShapeDtypeStruct((own_rows, columns), f32),
            jax.ShapeDtypeStruct((own_rows, columns), f32),
            jax.ShapeDtypeStruct((chips, own_rows, columns), bf16),
        ),
        in_specs=[IN_VMEM] * 3,
        out_specs=(IN_VMEM,) * 3,
        compiler_params=params(),
        cost_estimate=cost(1 << 20, 2 << 20),
    )(terms, first_moment, second_moment)
    mine = lax.all_to_all(copies, "chip", 0, 0, tiled=True)
    other = lax.ppermute(mine, "core", SWAP)
    expanded = pl.pallas_call(
        expand,
        out_shape=jax.ShapeDtypeStruct((features // 2, columns), bf16),
        in_specs=[IN_SMEM, IN_VMEM, IN_VMEM, IN_VMEM],
        out_specs=IN_VMEM,
        scratch_shapes=[pltpu.VMEM((chips, 2, own_rows, columns), bf16)],
        compiler_params=params(),
        cost_estimate=cost(features * rank * columns, 4 << 20),
    )(core, summed, mine, other)
    return (moment_next, square_next, expanded)


def solution(mesh):
    devices = np.asarray(mesh.devices)
    inner = Mesh(devices.reshape(devices.shape[0] // 2, 2, devices.shape[1]), ("chip", "core", "fsdp"))
    split = P(("chip", "core"), "fsdp")
    in_specs = (split, split, P("fsdp", None), split, split)
    return jax.shard_map(body, mesh=inner, in_specs=in_specs, out_specs=(split, split, split), check_vma=False)
```

```python
import numpy as np
import jax
import jax.numpy as jnp
from jax import lax
from jax.experimental import pallas as pl
from jax.experimental.pallas import tpu as pltpu
from jax.sharding import Mesh, PartitionSpec as P

decay_first = 0.9
decay_second = 0.999
epsilon = 1e-08

SWAP = [(0, 1), (1, 0)]
VMEM_LIMIT = 40 * 1024 * 1024
LAST = (((1,), (1,)), ((), ()))
IN_VMEM = pl.BlockSpec(memory_space=pltpu.VMEM)
IN_HBM = pl.BlockSpec(memory_space=pltpu.HBM)
IN_SMEM = pl.BlockSpec(memory_space=pltpu.SMEM)


def params(limit=VMEM_LIMIT):
    return pltpu.CompilerParams(vmem_limit_bytes=limit)


def cost(flops, moved):
    return pl.CostEstimate(flops=flops, bytes_accessed=moved, transcendentals=0)


def project(own_rows, core_ref, holds_ref, basis_hbm, own_hbm, other_hbm, out_hbm, rest_hbm, basis_ref, own_ref, other_ref, out_ref, sems):
    features, rank = basis_ref.shape
    tokens = own_ref.shape[0]
    half = rank // 2
    rows = features // 4
    parts = half // rows
    wide = rank // parts
    load_basis = pltpu.make_async_copy(basis_hbm, basis_ref, sems.at[0])
    load_own = pltpu.make_async_copy(own_hbm, own_ref, sems.at[1])
    load_basis.start()
    load_own.start()
    load_other = pltpu.make_async_copy(other_hbm, other_ref, sems.at[2])
    load_other.start()
    at = lax.broadcasted_iota(jnp.int32, (half, rank), 0)
    wanted = at // own_rows * (2 * own_rows) + core_ref[0] * own_rows + at % own_rows
    pick = (lax.broadcasted_iota(jnp.int32, (half, rank), 1) == wanted).astype(jnp.bfloat16)
    load_basis.wait()
    picked = lax.dot_general(pick, basis_ref[...], LAST, preferred_element_type=jnp.float32).astype(jnp.bfloat16)
    saves = []

    def save(start, size):
        here = pl.ds(start, size)
        saves.append(pltpu.make_async_copy(out_ref.at[:, here], out_hbm.at[:, here], sems.at[3 + len(saves)]))
        saves[-1].start()

    load_own.wait()
    out_ref[:, :tokens] = lax.dot_general(picked, own_ref[...], LAST, preferred_element_type=jnp.float32)
    save(0, tokens)
    load_other.wait()
    out_ref[:, tokens : 2 * tokens] = lax.dot_general(picked, other_ref[...], LAST, preferred_element_type=jnp.float32)
    save(tokens, tokens)
    mine = basis_ref[pl.ds(pl.multiple_of(core_ref[0] * (2 * rows), rows), rows), :].astype(jnp.float32)
    mine = jnp.where(holds_ref[0] == 1, mine, 0.0)
    for i in range(parts):
        out_ref[i * rows : (i + 1) * rows, 2 * tokens :] = mine[:, i * wide : (i + 1) * wide]
    save(2 * tokens, wide)
    rest = pl.ds(pl.multiple_of((2 * core_ref[0] + 1) * rows, rows), rows)
    saves.append(pltpu.make_async_copy(basis_ref.at[rest, :], rest_hbm, sems.at[6]))
    saves[-1].start()
    for copy in saves:
        copy.wait()


def grad_terms(summed_ref, own_ref, other_hbm, _, out_hbm, rest_hbm, other_ref, total_ref, out_ref, sems):
    tokens = own_ref.shape[0]
    first = tokens // 3 * 2
    loads = []
    for i, (start, size) in enumerate(((0, first), (first, tokens - first))):
        rows = pl.ds(start, size)
        loads.append(pltpu.make_async_copy(other_hbm.at[rows, :], other_ref.at[rows, :], sems.at[i]))
        loads[i].start()
    total_ref[...] = jnp.dot(summed_ref[:, :tokens], own_ref[...], preferred_element_type=jnp.float32)
    for load in loads:
        load.wait()
    part = out_ref.shape[0] // 2
    saves = []
    for i in range(2):
        rows = pl.ds(i * part, part)
        more = jnp.dot(summed_ref[rows, tokens : 2 * tokens], other_ref[...], preferred_element_type=jnp.float32)
        out_ref[rows, :] = (total_ref[rows, :] + more).astype(jnp.bfloat16)
        saves.append(pltpu.make_async_copy(out_ref.at[rows, :], out_hbm.at[rows, :], sems.at[2 + i]))
        saves[i].start()
    for save in saves:
        save.wait()


def adam(terms_ref, first_ref, second_ref, _, moment_ref, square_ref, copies_ref):
    gradient = terms_ref[0].astype(jnp.float32)
    for i in range(1, terms_ref.shape[0]):
        gradient += terms_ref[i].astype(jnp.float32)
    moment_next = decay_first * first_ref[...] + (1.0 - decay_first) * gradient
    square_next = decay_second * second_ref[...] + (1.0 - decay_second) * gradient * gradient
    moment_ref[...] = moment_next
    square_ref[...] = square_next
    direction = (moment_next / (jnp.sqrt(square_next) + epsilon)).astype(jnp.bfloat16)
    for i in range(copies_ref.shape[0]):
        copies_ref[i] = direction


def expand(core_ref, summed_ref, rest_ref, mine_ref, other_ref, out_ref, block_ref, all_ref):
    rows = rest_ref.shape[0]
    rank = block_ref.shape[1]
    parts = summed_ref.shape[0] // rows
    wide = rank // parts
    start = summed_ref.shape[1] - wide
    core = core_ref[0]
    for i in range(parts):
        block_ref[:rows, i * wide : (i + 1) * wide] = summed_ref[i * rows : (i + 1) * rows, start:]
    block_ref[rows:, :] = rest_ref[...]
    all_ref[:, pl.ds(core, 1)] = mine_ref[...][:, None]
    all_ref[:, pl.ds(1 - core, 1)] = other_ref[...][:, None]
    direction = all_ref[...].reshape(rank, out_ref.shape[1])
    out_ref[...] = jnp.dot(block_ref[...], direction, preferred_element_type=jnp.float32).astype(jnp.bfloat16)


def block_pairs(chips):
    pairs = []
    for p in range(chips):
        for k in range(chips):
            z = (k + p // 4 + 4 * ((p + k) % 4)) % chips
            pairs += [((p * 2 + c) * chips + k, (k * 2 + c) * chips + z) for c in range(2)]
    return pairs


def body(activations, cotangent, basis, first_moment, second_moment):
    chips = lax.axis_size("chip")
    features, rank = basis.shape
    tokens = activations.shape[0]
    half = rank // 2
    rows = features // 4
    width = 2 * tokens + rank * rows // half
    own_rows, columns = first_moment.shape
    core = lax.axis_index("core").astype(jnp.int32).reshape(1)
    holds = (lax.axis_index("chip") == lax.axis_index("fsdp")).astype(jnp.int32).reshape(1)
    f32, bf16 = jnp.float32, jnp.bfloat16

    other_act = lax.ppermute(activations, "core", SWAP)
    other_cot = lax.ppermute(cotangent, "core", SWAP)
    partial, rest = pl.pallas_call(
        lambda *refs: project(own_rows, *refs),
        out_shape=(pltpu.HBM((half, width), f32), pltpu.HBM((rows, rank), bf16)),
        in_specs=[IN_SMEM, IN_SMEM, IN_HBM, IN_HBM, IN_HBM],
        out_specs=(IN_HBM, IN_HBM),
        scratch_shapes=[
            pltpu.VMEM((features, rank), bf16),
            pltpu.VMEM((tokens, features), bf16),
            pltpu.VMEM((tokens, features), bf16),
            pltpu.VMEM((half, width), f32),
            pltpu.SemaphoreType.DMA((7,)),
        ],
        compiler_params=params(55 * 1024 * 1024),
        cost_estimate=cost(3 * rank * tokens * features, 7 << 20),
    )(core, holds, basis, activations, other_act)
    summed = lax.psum(partial, "fsdp").astype(bf16)

    terms, rest = pl.pallas_call(
        grad_terms,
        out_shape=(pltpu.HBM((half, columns), bf16), pltpu.HBM((rows, rank), bf16)),
        in_specs=[IN_VMEM, IN_VMEM, IN_HBM, IN_HBM],
        out_specs=(IN_HBM, IN_HBM),
        input_output_aliases={3: 1},
        scratch_shapes=[
            pltpu.VMEM((tokens, columns), bf16),
            pltpu.VMEM((half, columns), f32),
            pltpu.VMEM((half, columns), bf16),
            pltpu.SemaphoreType.DMA((4,)),
        ],
        compiler_params=params(),
        cost_estimate=cost(2 * rank * tokens * columns, 5 << 20),
    )(summed, cotangent, other_cot, rest)
    rest = lax.ppermute(rest, ("chip", "core", "fsdp"), block_pairs(chips))
    terms = lax.all_to_all(terms.reshape(chips, own_rows, columns), "chip", 0, 0, tiled=True)

    moment_next, square_next, copies = pl.pallas_call(
        adam,
        out_shape=(
            jax.ShapeDtypeStruct((own_rows, columns), f32),
            jax.ShapeDtypeStruct((own_rows, columns), f32),
            jax.ShapeDtypeStruct((chips, own_rows, columns), bf16),
        ),
        in_specs=[IN_VMEM] * 3 + [IN_HBM],
        out_specs=(IN_VMEM,) * 3,
        compiler_params=params(),
        cost_estimate=cost(1 << 20, 2 << 20),
    )(terms, first_moment, second_moment, rest)
    mine = lax.all_to_all(copies, "chip", 0, 0, tiled=True)
    other = lax.ppermute(mine, "core", SWAP)
    expanded = pl.pallas_call(
        expand,
        out_shape=jax.ShapeDtypeStruct((features // 2, columns), bf16),
        in_specs=[IN_SMEM] + [IN_VMEM] * 4,
        out_specs=IN_VMEM,
        scratch_shapes=[pltpu.VMEM((2 * rows, rank), bf16), pltpu.VMEM((chips, 2, own_rows, columns), bf16)],
        compiler_params=params(),
        cost_estimate=cost(features * rank * columns, 4 << 20),
    )(core, summed, rest, mine, other)
    return (moment_next, square_next, expanded)


def solution(mesh):
    devices = np.asarray(mesh.devices)
    inner = Mesh(devices.reshape(devices.shape[0] // 2, 2, devices.shape[1]), ("chip", "core", "fsdp"))
    split = P(("chip", "core"), "fsdp")
    in_specs = (split, split, P("fsdp", None), split, split)
    return jax.shard_map(body, mesh=inner, in_specs=in_specs, out_specs=(split, split, split), check_vma=False)
```

```python
import numpy as np
import jax
import jax.numpy as jnp
from jax import lax
from jax.experimental import pallas as pl
from jax.experimental.pallas import tpu as pltpu
from jax.sharding import Mesh, PartitionSpec as P

decay_first = 0.9
decay_second = 0.999
epsilon = 1e-08

SWAP = [(0, 1), (1, 0)]
VMEM_LIMIT = 40 * 1024 * 1024
LAST = (((1,), (1,)), ((), ()))
IN_VMEM = pl.BlockSpec(memory_space=pltpu.VMEM)
IN_HBM = pl.BlockSpec(memory_space=pltpu.HBM)
IN_SMEM = pl.BlockSpec(memory_space=pltpu.SMEM)


def params(limit=VMEM_LIMIT):
    return pltpu.CompilerParams(vmem_limit_bytes=limit)


def cost(flops, moved):
    return pl.CostEstimate(flops=flops, bytes_accessed=moved, transcendentals=0)


def project(core_ref, holds_ref, basis_hbm, act_hbm, out_hbm, basis_ref, act_ref, out_ref, sems):
    features, rank = basis_ref.shape
    tokens = act_ref.shape[0]
    rows = features // 2
    parts = rank // rows
    wide = rank // parts
    load_basis = pltpu.make_async_copy(basis_hbm, basis_ref, sems.at[0])
    load_act = pltpu.make_async_copy(act_hbm, act_ref, sems.at[1])
    load_basis.start()
    load_act.start()
    load_basis.wait()
    mine = basis_ref[pl.ds(pl.multiple_of(core_ref[0] * rows, rows), rows), :].astype(jnp.float32)
    mine = jnp.where(holds_ref[0] == 1, mine, 0.0)
    for i in range(parts):
        out_ref[i * rows : (i + 1) * rows, tokens:] = mine[:, i * wide : (i + 1) * wide]
    load_act.wait()
    saves = []
    for i in range(parts):
        here = pl.ds(i * rows, rows)
        some = basis_ref[:, i * rows : (i + 1) * rows].T
        out_ref[here, :tokens] = lax.dot_general(some, act_ref[...], LAST, preferred_element_type=jnp.float32)
        saves.append(pltpu.make_async_copy(out_ref.at[here, :], out_hbm.at[here, :], sems.at[2 + i]))
        saves[i].start()
    for copy in saves:
        copy.wait()


def half_terms(sibling, core_ref, summed_ref, cot_ref, out_ref):
    tokens = cot_ref.shape[0]
    side = 1 - core_ref[0] if sibling else core_ref[0]
    projected = summed_ref[:, pl.ds(side, 1), :, :tokens].reshape(out_ref.shape[0], tokens)
    out_ref[...] = jnp.dot(projected, cot_ref[...], preferred_element_type=jnp.float32).astype(out_ref.dtype)


def add_terms(kept_ref, got_ref, out_ref):
    out_ref[...] = (kept_ref[...] + got_ref[...].astype(jnp.float32)).astype(jnp.bfloat16)


def adam(terms_ref, first_ref, second_ref, moment_ref, square_ref, copies_ref):
    gradient = terms_ref[0].astype(jnp.float32)
    for i in range(1, terms_ref.shape[0]):
        gradient += terms_ref[i].astype(jnp.float32)
    moment_next = decay_first * first_ref[...] + (1.0 - decay_first) * gradient
    square_next = decay_second * second_ref[...] + (1.0 - decay_second) * gradient * gradient
    moment_ref[...] = moment_next
    square_ref[...] = square_next
    direction = (moment_next / (jnp.sqrt(square_next) + epsilon)).astype(jnp.bfloat16)
    for i in range(copies_ref.shape[0]):
        copies_ref[i] = direction


def expand(core_ref, summed_ref, mine_ref, other_ref, out_ref, block_ref, all_ref):
    rows, columns = out_ref.shape
    rank = block_ref.shape[1]
    parts = summed_ref.shape[0] // rows
    wide = rank // parts
    start = summed_ref.shape[1] - wide
    core = core_ref[0]
    for i in range(parts):
        block_ref[:, i * wide : (i + 1) * wide] = summed_ref[i * rows : (i + 1) * rows, start:]
    all_ref[:, pl.ds(core, 1)] = mine_ref[...][:, None]
    all_ref[:, pl.ds(1 - core, 1)] = other_ref[...][:, None]
    direction = all_ref[...].reshape(rank, columns)
    out_ref[...] = jnp.dot(block_ref[...], direction, preferred_element_type=jnp.float32).astype(jnp.bfloat16)


def body(activations, cotangent, basis, first_moment, second_moment):
    chips = lax.axis_size("chip")
    features, rank = basis.shape
    tokens = activations.shape[0]
    half = rank // 2
    own_rows, columns = first_moment.shape
    core = lax.axis_index("core").astype(jnp.int32).reshape(1)
    holds = (lax.axis_index("chip") == lax.axis_index("fsdp")).astype(jnp.int32).reshape(1)
    f32, bf16 = jnp.float32, jnp.bfloat16

    rows = features // 2
    width = tokens + rows
    partial = pl.pallas_call(
        project,
        out_shape=pltpu.HBM((rank, width), f32),
        in_specs=[IN_SMEM, IN_SMEM, IN_HBM, IN_HBM],
        out_specs=IN_HBM,
        scratch_shapes=[
            pltpu.VMEM((features, rank), bf16),
            pltpu.VMEM((tokens, features), bf16),
            pltpu.VMEM((rank, width), f32),
            pltpu.SemaphoreType.DMA((2 + rank // rows,)),
        ],
        compiler_params=params(55 * 1024 * 1024),
        cost_estimate=cost(2 * rank * tokens * features, 6 << 20),
    )(core, holds, basis, activations)
    summed = lax.psum(partial, "fsdp").astype(bf16)

    def half_of(sibling, dtype):
        return pl.pallas_call(
            lambda *refs: half_terms(sibling, *refs),
            out_shape=jax.ShapeDtypeStruct((half, columns), dtype),
            in_specs=[IN_SMEM, IN_VMEM, IN_VMEM],
            out_specs=IN_VMEM,
            compiler_params=params(),
            cost_estimate=cost(rank * tokens * columns, 4 << 20),
        )(core, summed.reshape(chips, 2, own_rows, width), cotangent)

    got = lax.ppermute(half_of(True, bf16), "core", SWAP)
    terms = pl.pallas_call(
        add_terms,
        out_shape=jax.ShapeDtypeStruct((half, columns), bf16),
        in_specs=[IN_VMEM] * 2,
        out_specs=IN_VMEM,
        compiler_params=params(),
        cost_estimate=cost(half * columns, 4 << 20),
    )(half_of(False, f32), got)
    terms = lax.all_to_all(terms.reshape(chips, own_rows, columns), "chip", 0, 0, tiled=True)

    moment_next, square_next, copies = pl.pallas_call(
        adam,
        out_shape=(
            jax.ShapeDtypeStruct((own_rows, columns), f32),
            jax.ShapeDtypeStruct((own_rows, columns), f32),
            jax.ShapeDtypeStruct((chips, own_rows, columns), bf16),
        ),
        in_specs=[IN_VMEM] * 3,
        out_specs=(IN_VMEM,) * 3,
        compiler_params=params(),
        cost_estimate=cost(1 << 20, 2 << 20),
    )(terms, first_moment, second_moment)
    mine = lax.all_to_all(copies, "chip", 0, 0, tiled=True)
    other = lax.ppermute(mine, "core", SWAP)
    expanded = pl.pallas_call(
        expand,
        out_shape=jax.ShapeDtypeStruct((features // 2, columns), bf16),
        in_specs=[IN_SMEM, IN_VMEM, IN_VMEM, IN_VMEM],
        out_specs=IN_VMEM,
        scratch_shapes=[pltpu.VMEM((rows, rank), bf16), pltpu.VMEM((chips, 2, own_rows, columns), bf16)],
        compiler_params=params(),
        cost_estimate=cost(features * rank * columns, 4 << 20),
    )(core, summed, mine, other)
    return (moment_next, square_next, expanded)


def solution(mesh):
    devices = np.asarray(mesh.devices)
    inner = Mesh(devices.reshape(devices.shape[0] // 2, 2, devices.shape[1]), ("chip", "core", "fsdp"))
    split = P(("chip", "core"), "fsdp")
    in_specs = (split, split, P("fsdp", None), split, split)
    return jax.shard_map(body, mesh=inner, in_specs=in_specs, out_specs=(split, split, split), check_vma=False)
```

```python
import numpy as np
import jax
import jax.numpy as jnp
from jax import lax
from jax.experimental import pallas as pl
from jax.experimental.pallas import tpu as pltpu
from jax.sharding import Mesh, PartitionSpec as P

decay_first = 0.9
decay_second = 0.999
epsilon = 1e-08

SWAP = [(0, 1), (1, 0)]
VMEM_LIMIT = 40 * 1024 * 1024
LAST = (((1,), (1,)), ((), ()))
IN_VMEM = pl.BlockSpec(memory_space=pltpu.VMEM)
IN_HBM = pl.BlockSpec(memory_space=pltpu.HBM)
IN_SMEM = pl.BlockSpec(memory_space=pltpu.SMEM)


def params(limit=VMEM_LIMIT):
    return pltpu.CompilerParams(vmem_limit_bytes=limit)


def cost(flops, moved):
    return pl.CostEstimate(flops=flops, bytes_accessed=moved, transcendentals=0)


def project_rows(picked, act_ref, out_ref, out_hbm, sems):
    part = out_ref.shape[0] // 2
    copies = []
    for i in range(2):
        rows = pl.ds(i * part, part)
        out_ref[rows, :] = lax.dot_general(
            picked[i * part : (i + 1) * part], act_ref[...], LAST, preferred_element_type=jnp.float32
        )
        copies.append(pltpu.make_async_copy(out_ref.at[rows, :], out_hbm.at[rows, :], sems.at[i]))
        copies[i].start()
    return copies


def project_own(core_ref, holds_ref, basis_hbm, act_hbm, out_hbm, picked_ref, basis_ref, act_ref, turned_ref, own_ref, block_ref, sems):
    features, rank = basis_ref.shape
    tokens = act_ref.shape[0]
    half = rank // 2
    rows = features // 2
    load_basis = pltpu.make_async_copy(basis_hbm, basis_ref, sems.at[0])
    load_act = pltpu.make_async_copy(act_hbm, act_ref, sems.at[1])
    load_basis.start()
    load_act.start()
    load_basis.wait()
    mine = basis_ref[pl.ds(pl.multiple_of(core_ref[0] * rows, rows), rows), :].astype(jnp.float32)
    mine = jnp.where(holds_ref[0] == 1, mine, 0.0)
    block_ref[:rows, :] = mine[:, :half]
    block_ref[rows:, :] = mine[:, half:]
    save_block = pltpu.make_async_copy(block_ref, out_hbm.at[:, pl.ds(2 * tokens, half)], sems.at[2])
    save_block.start()
    turned_ref[...] = basis_ref[...].T.reshape(turned_ref.shape)
    picked = turned_ref[:, pl.ds(core_ref[0], 1)].reshape(half, features)
    picked_ref[...] = picked
    load_act.wait()
    copies = project_rows(picked, act_ref, own_ref, out_hbm.at[:, pl.ds(0, tokens)], sems.at[pl.ds(3, 2)])
    for copy in [save_block] + copies:
        copy.wait()


def project_other(picked_ref, act_ref, _, out_hbm, other_ref, sems):
    tokens = act_ref.shape[0]
    copies = project_rows(picked_ref[...], act_ref, other_ref, out_hbm.at[:, pl.ds(tokens, tokens)], sems)
    for copy in copies:
        copy.wait()


def grad_terms(summed_ref, own_ref, other_hbm, out_ref, other_ref, total_ref, sems):
    tokens = own_ref.shape[0]
    part = tokens // 2
    loads = []
    for i in range(2):
        rows = pl.ds(i * part, part)
        loads.append(pltpu.make_async_copy(other_hbm.at[rows, :], other_ref.at[rows, :], sems.at[i]))
        loads[i].start()
    total_ref[...] = jnp.dot(summed_ref[:, :tokens], own_ref[...], preferred_element_type=jnp.float32)
    for load in loads:
        load.wait()
    part = out_ref.shape[0] // 2
    for i in range(2):
        rows = pl.ds(i * part, part)
        more = jnp.dot(summed_ref[rows, tokens : 2 * tokens], other_ref[...], preferred_element_type=jnp.float32)
        out_ref[rows, :] = (total_ref[rows, :] + more).astype(jnp.bfloat16)


def adam(terms_ref, first_ref, second_ref, moment_ref, square_ref, copies_ref):
    gradient = terms_ref[0].astype(jnp.float32)
    for i in range(1, terms_ref.shape[0]):
        gradient += terms_ref[i].astype(jnp.float32)
    moment_next = decay_first * first_ref[...] + (1.0 - decay_first) * gradient
    square_next = decay_second * second_ref[...] + (1.0 - decay_second) * gradient * gradient
    moment_ref[...] = moment_next
    square_ref[...] = square_next
    direction = (moment_next / (jnp.sqrt(square_next) + epsilon)).astype(jnp.bfloat16)
    for i in range(copies_ref.shape[0]):
        copies_ref[i] = direction


def expand(core_ref, summed_ref, mine_ref, other_ref, out_ref, all_ref):
    rows, columns = out_ref.shape
    half = summed_ref.shape[0]
    start = summed_ref.shape[1] - half
    core = core_ref[0]
    all_ref[:, pl.ds(core, 1)] = mine_ref[...][:, None]
    all_ref[:, pl.ds(1 - core, 1)] = other_ref[...][:, None]
    direction = all_ref[...].reshape(2 * half, columns)
    total = jnp.dot(summed_ref[:rows, start:], direction[:half], preferred_element_type=jnp.float32)
    total += jnp.dot(summed_ref[rows:, start:], direction[half:], preferred_element_type=jnp.float32)
    out_ref[...] = total.astype(jnp.bfloat16)


def body(activations, cotangent, basis, first_moment, second_moment):
    chips = lax.axis_size("chip")
    features, rank = basis.shape
    tokens = activations.shape[0]
    half = rank // 2
    own_rows, columns = first_moment.shape
    core = lax.axis_index("core").astype(jnp.int32).reshape(1)
    holds = (lax.axis_index("chip") == lax.axis_index("fsdp")).astype(jnp.int32).reshape(1)
    f32, bf16 = jnp.float32, jnp.bfloat16

    other_act = lax.ppermute(activations, "core", SWAP)
    other_cot = lax.ppermute(cotangent, "core", SWAP)
    width = 2 * tokens + half
    partial, picked = pl.pallas_call(
        project_own,
        out_shape=(pltpu.HBM((half, width), f32), pltpu.VMEM((half, features), bf16)),
        in_specs=[IN_SMEM, IN_SMEM, IN_HBM, IN_HBM],
        out_specs=(IN_HBM, IN_VMEM),
        scratch_shapes=[
            pltpu.VMEM((features, rank), bf16),
            pltpu.VMEM((tokens, features), bf16),
            pltpu.VMEM((chips, 2, own_rows, features), bf16),
            pltpu.VMEM((half, tokens), f32),
            pltpu.VMEM((half, half), f32),
            pltpu.SemaphoreType.DMA((5,)),
        ],
        compiler_params=params(60 * 1024 * 1024),
        cost_estimate=cost(2 * rank * tokens * features, 5 << 20),
    )(core, holds, basis, activations)
    partial = pl.pallas_call(
        project_other,
        out_shape=pltpu.HBM((half, width), f32),
        in_specs=[IN_VMEM, IN_VMEM, IN_HBM],
        out_specs=IN_HBM,
        scratch_shapes=[pltpu.VMEM((half, tokens), f32), pltpu.SemaphoreType.DMA((2,))],
        input_output_aliases={2: 0},
        compiler_params=params(),
        cost_estimate=cost(rank * tokens * features, 3 << 20),
    )(picked, other_act, partial)
    summed = lax.psum(partial, "fsdp").astype(bf16)

    terms = pl.pallas_call(
        grad_terms,
        out_shape=jax.ShapeDtypeStruct((half, columns), bf16),
        in_specs=[IN_VMEM, IN_VMEM, IN_HBM],
        out_specs=IN_VMEM,
        scratch_shapes=[
            pltpu.VMEM((tokens, columns), bf16),
            pltpu.VMEM((half, columns), f32),
            pltpu.SemaphoreType.DMA((2,)),
        ],
        compiler_params=params(),
        cost_estimate=cost(2 * rank * tokens * columns, 5 << 20),
    )(summed, cotangent, other_cot)
    terms = lax.all_to_all(terms.reshape(chips, own_rows, columns), "chip", 0, 0, tiled=True)

    moment_next, square_next, copies = pl.pallas_call(
        adam,
        out_shape=(
            jax.ShapeDtypeStruct((own_rows, columns), f32),
            jax.ShapeDtypeStruct((own_rows, columns), f32),
            jax.ShapeDtypeStruct((chips, own_rows, columns), bf16),
        ),
        in_specs=[IN_VMEM] * 3,
        out_specs=(IN_VMEM,) * 3,
        compiler_params=params(),
        cost_estimate=cost(1 << 20, 2 << 20),
    )(terms, first_moment, second_moment)
    mine = lax.all_to_all(copies, "chip", 0, 0, tiled=True)
    other = lax.ppermute(mine, "core", SWAP)
    expanded = pl.pallas_call(
        expand,
        out_shape=jax.ShapeDtypeStruct((features // 2, columns), bf16),
        in_specs=[IN_SMEM, IN_VMEM, IN_VMEM, IN_VMEM],
        out_specs=IN_VMEM,
        scratch_shapes=[pltpu.VMEM((chips, 2, own_rows, columns), bf16)],
        compiler_params=params(),
        cost_estimate=cost(features * rank * columns, 4 << 20),
    )(core, summed, mine, other)
    return (moment_next, square_next, expanded)


def solution(mesh):
    devices = np.asarray(mesh.devices)
    inner = Mesh(devices.reshape(devices.shape[0] // 2, 2, devices.shape[1]), ("chip", "core", "fsdp"))
    split = P(("chip", "core"), "fsdp")
    in_specs = (split, split, P("fsdp", None), split, split)
    return jax.shard_map(body, mesh=inner, in_specs=in_specs, out_specs=(split, split, split), check_vma=False)
```

```python
import numpy as np
import jax
import jax.numpy as jnp
from jax import lax
from jax.experimental import pallas as pl
from jax.experimental.pallas import tpu as pltpu
from jax.sharding import Mesh, PartitionSpec as P

decay_first = 0.9
decay_second = 0.999
epsilon = 1e-08

SWAP = [(0, 1), (1, 0)]
VMEM_LIMIT = 40 * 1024 * 1024
LAST = (((1,), (1,)), ((), ()))
IN_VMEM = pl.BlockSpec(memory_space=pltpu.VMEM)
IN_HBM = pl.BlockSpec(memory_space=pltpu.HBM)
IN_SMEM = pl.BlockSpec(memory_space=pltpu.SMEM)


def params(limit=VMEM_LIMIT):
    return pltpu.CompilerParams(vmem_limit_bytes=limit)


def cost(flops, moved):
    return pl.CostEstimate(flops=flops, bytes_accessed=moved, transcendentals=0)


def project_rows(picked, act_ref, out_ref, out_hbm, sems):
    part = out_ref.shape[0] // 2
    copies = []
    for i in range(2):
        rows = pl.ds(i * part, part)
        out_ref[rows, :] = lax.dot_general(
            picked[i * part : (i + 1) * part], act_ref[...], LAST, preferred_element_type=jnp.float32
        )
        copies.append(pltpu.make_async_copy(out_ref.at[rows, :], out_hbm.at[rows, :], sems.at[i]))
        copies[i].start()
    return copies


def project_own(core_ref, holds_ref, basis_hbm, act_hbm, out_hbm, picked_ref, basis_ref, act_ref, turned_ref, own_ref, block_ref, sems):
    features, rank = basis_ref.shape
    tokens = act_ref.shape[0]
    half = rank // 2
    rows = features // 2
    load_basis = pltpu.make_async_copy(basis_hbm, basis_ref, sems.at[0])
    load_act = pltpu.make_async_copy(act_hbm, act_ref, sems.at[1])
    load_basis.start()
    load_act.start()
    load_basis.wait()
    mine = basis_ref[pl.ds(pl.multiple_of(core_ref[0] * rows, rows), rows), :].astype(jnp.float32)
    mine = jnp.where(holds_ref[0] == 1, mine, 0.0)
    block_ref[:rows, :] = mine[:, :half]
    block_ref[rows:, :] = mine[:, half:]
    save_block = pltpu.make_async_copy(block_ref, out_hbm.at[:, pl.ds(2 * tokens, half)], sems.at[2])
    save_block.start()
    turned_ref[...] = basis_ref[...].T.reshape(turned_ref.shape)
    picked = turned_ref[:, pl.ds(core_ref[0], 1)].reshape(half, features)
    picked_ref[...] = picked
    load_act.wait()
    copies = project_rows(picked, act_ref, own_ref, out_hbm.at[:, pl.ds(0, tokens)], sems.at[pl.ds(3, 2)])
    for copy in [save_block] + copies:
        copy.wait()


def project_other(picked_ref, act_ref, _, out_hbm, other_ref, sems):
    tokens = act_ref.shape[0]
    copies = project_rows(picked_ref[...], act_ref, other_ref, out_hbm.at[:, pl.ds(tokens, tokens)], sems)
    for copy in copies:
        copy.wait()


def own_terms(summed_ref, own_ref, other_hbm, out_ref, other_ref, sem):
    tokens = own_ref.shape[0]
    load = pltpu.make_async_copy(other_hbm, other_ref, sem)
    load.start()
    out_ref[...] = jnp.dot(summed_ref[:, :tokens], own_ref[...], preferred_element_type=jnp.float32)
    load.wait()


def all_terms(own_ref, summed_ref, other_ref, out_ref):
    tokens = other_ref.shape[0]
    more = jnp.dot(summed_ref[:, tokens : 2 * tokens], other_ref[...], preferred_element_type=jnp.float32)
    out_ref[...] = (own_ref[...] + more).astype(jnp.bfloat16)


def adam(terms_ref, first_ref, second_ref, moment_ref, square_ref, copies_ref):
    gradient = terms_ref[0].astype(jnp.float32)
    for i in range(1, terms_ref.shape[0]):
        gradient += terms_ref[i].astype(jnp.float32)
    moment_next = decay_first * first_ref[...] + (1.0 - decay_first) * gradient
    square_next = decay_second * second_ref[...] + (1.0 - decay_second) * gradient * gradient
    moment_ref[...] = moment_next
    square_ref[...] = square_next
    direction = (moment_next / (jnp.sqrt(square_next) + epsilon)).astype(jnp.bfloat16)
    for i in range(copies_ref.shape[0]):
        copies_ref[i] = direction


def expand_own(core_ref, summed_ref, mine_ref, out_ref, rest_ref):
    rows, half = rest_ref.shape
    own_rows = mine_ref.shape[1]
    start = summed_ref.shape[1] - half
    left, right = summed_ref[:rows, start:], summed_ref[rows:, start:]

    def columns_of(side):
        at = lax.broadcasted_iota(jnp.int32, (half // 2, half), 0)
        wanted = at // own_rows * (2 * own_rows) + side * own_rows + at % own_rows
        pick = (lax.broadcasted_iota(jnp.int32, (half // 2, half), 1) == wanted).astype(jnp.bfloat16)
        picked = [lax.dot_general(part, pick, LAST, preferred_element_type=jnp.float32) for part in (left, right)]
        return jnp.concatenate(picked, 1).astype(jnp.bfloat16)

    direction = mine_ref[...].reshape(half, mine_ref.shape[2])
    out_ref[...] = jnp.dot(columns_of(core_ref[0]), direction, preferred_element_type=jnp.float32)
    rest_ref[...] = columns_of(1 - core_ref[0])


def expand(own_ref, rest_ref, other_ref, out_ref):
    direction = other_ref[...].reshape(rest_ref.shape[1], other_ref.shape[2])
    more = jnp.dot(rest_ref[...], direction, preferred_element_type=jnp.float32)
    out_ref[...] = (own_ref[...] + more).astype(jnp.bfloat16)


def body(activations, cotangent, basis, first_moment, second_moment):
    chips = lax.axis_size("chip")
    features, rank = basis.shape
    tokens = activations.shape[0]
    half = rank // 2
    own_rows, columns = first_moment.shape
    core = lax.axis_index("core").astype(jnp.int32).reshape(1)
    holds = (lax.axis_index("chip") == lax.axis_index("fsdp")).astype(jnp.int32).reshape(1)
    f32, bf16 = jnp.float32, jnp.bfloat16

    other_act = lax.ppermute(activations, "core", SWAP)
    other_cot = lax.ppermute(cotangent, "core", SWAP)
    width = 2 * tokens + half
    partial, picked = pl.pallas_call(
        project_own,
        out_shape=(pltpu.HBM((half, width), f32), pltpu.VMEM((half, features), bf16)),
        in_specs=[IN_SMEM, IN_SMEM, IN_HBM, IN_HBM],
        out_specs=(IN_HBM, IN_VMEM),
        scratch_shapes=[
            pltpu.VMEM((features, rank), bf16),
            pltpu.VMEM((tokens, features), bf16),
            pltpu.VMEM((chips, 2, own_rows, features), bf16),
            pltpu.VMEM((half, tokens), f32),
            pltpu.VMEM((half, half), f32),
            pltpu.SemaphoreType.DMA((5,)),
        ],
        compiler_params=params(60 * 1024 * 1024),
        cost_estimate=cost(2 * rank * tokens * features, 5 << 20),
    )(core, holds, basis, activations)
    partial = pl.pallas_call(
        project_other,
        out_shape=pltpu.HBM((half, width), f32),
        in_specs=[IN_VMEM, IN_VMEM, IN_HBM],
        out_specs=IN_HBM,
        scratch_shapes=[pltpu.VMEM((half, tokens), f32), pltpu.SemaphoreType.DMA((2,))],
        input_output_aliases={2: 0},
        compiler_params=params(),
        cost_estimate=cost(rank * tokens * features, 3 << 20),
    )(picked, other_act, partial)
    summed = lax.psum(partial, "fsdp").astype(bf16)

    own, other = pl.pallas_call(
        own_terms,
        out_shape=(pltpu.VMEM((half, columns), f32), pltpu.VMEM((tokens, columns), bf16)),
        in_specs=[IN_VMEM, IN_VMEM, IN_HBM],
        out_specs=(IN_VMEM, IN_VMEM),
        scratch_shapes=[pltpu.SemaphoreType.DMA],
        compiler_params=params(),
        cost_estimate=cost(rank * tokens * columns, 4 << 20),
    )(summed, cotangent, other_cot)
    terms = pl.pallas_call(
        all_terms,
        out_shape=jax.ShapeDtypeStruct((half, columns), bf16),
        in_specs=[IN_VMEM] * 3,
        out_specs=IN_VMEM,
        compiler_params=params(),
        cost_estimate=cost(rank * tokens * columns, 4 << 20),
    )(own, summed, other)
    terms = lax.all_to_all(terms.reshape(chips, own_rows, columns), "chip", 0, 0, tiled=True)

    moment_next, square_next, copies = pl.pallas_call(
        adam,
        out_shape=(
            jax.ShapeDtypeStruct((own_rows, columns), f32),
            jax.ShapeDtypeStruct((own_rows, columns), f32),
            jax.ShapeDtypeStruct((chips, own_rows, columns), bf16),
        ),
        in_specs=[IN_VMEM] * 3,
        out_specs=(IN_VMEM,) * 3,
        compiler_params=params(),
        cost_estimate=cost(1 << 20, 2 << 20),
    )(terms, first_moment, second_moment)
    mine = lax.all_to_all(copies, "chip", 0, 0, tiled=True)
    other = lax.ppermute(mine, "core", SWAP)
    rows = features // 2
    own, rest = pl.pallas_call(
        expand_own,
        out_shape=(pltpu.VMEM((rows, columns), f32), pltpu.VMEM((rows, half), bf16)),
        in_specs=[IN_SMEM, IN_VMEM, IN_VMEM],
        out_specs=(IN_VMEM, IN_VMEM),
        compiler_params=params(),
        cost_estimate=cost(rows * rank * columns, 3 << 20),
    )(core, summed, mine)
    expanded = pl.pallas_call(
        expand,
        out_shape=jax.ShapeDtypeStruct((rows, columns), bf16),
        in_specs=[IN_VMEM] * 3,
        out_specs=IN_VMEM,
        compiler_params=params(),
        cost_estimate=cost(rows * rank * columns, 3 << 20),
    )(own, rest, other)
    return (moment_next, square_next, expanded)


def solution(mesh):
    devices = np.asarray(mesh.devices)
    inner = Mesh(devices.reshape(devices.shape[0] // 2, 2, devices.shape[1]), ("chip", "core", "fsdp"))
    split = P(("chip", "core"), "fsdp")
    in_specs = (split, split, P("fsdp", None), split, split)
    return jax.shard_map(body, mesh=inner, in_specs=in_specs, out_specs=(split, split, split), check_vma=False)
```

```python
import numpy as np
import jax
import jax.numpy as jnp
from jax import lax
from jax.experimental import pallas as pl
from jax.experimental.pallas import tpu as pltpu
from jax.sharding import Mesh, PartitionSpec as P

decay_first = 0.9
decay_second = 0.999
epsilon = 1e-08

SWAP = [(0, 1), (1, 0)]
VMEM_LIMIT = 40 * 1024 * 1024
GRAD_LIMIT = 40 * 1024 * 1024
LANES = 128
LAST = (((1,), (1,)), ((), ()))
IN_VMEM = pl.BlockSpec(memory_space=pltpu.VMEM)
IN_HBM = pl.BlockSpec(memory_space=pltpu.HBM)
IN_SMEM = pl.BlockSpec(memory_space=pltpu.SMEM)


def params(limit=VMEM_LIMIT):
    return pltpu.CompilerParams(vmem_limit_bytes=limit)


def cost(flops, moved):
    return pl.CostEstimate(flops=flops, bytes_accessed=moved, transcendentals=0)


def give_pieces(core_ref, chip_ref, basis_hbm, out_hbm, sems):
    count, rows, _ = out_hbm.shape
    start = pl.multiple_of(core_ref[0] * (basis_hbm.shape[0] // 2) + chip_ref[0] * rows, rows)
    copies = []
    for i in range(count):
        copies.append(pltpu.make_async_copy(basis_hbm.at[pl.ds(start, rows), :], out_hbm.at[i], sems.at[i]))
        copies[i].start()
    for copy in copies:
        copy.wait()


def project_rows(picked, act_ref, out_ref, out_hbm, sems):
    part = out_ref.shape[0] // 2
    copies = []
    for i in range(2):
        rows = pl.ds(i * part, part)
        out_ref[rows, :] = lax.dot_general(
            picked[i * part : (i + 1) * part], act_ref[...], LAST, preferred_element_type=jnp.float32
        )
        copies.append(pltpu.make_async_copy(out_ref.at[rows, :], out_hbm.at[rows, :], sems.at[i]))
        copies[i].start()
    return copies


def project_own(core_ref, basis_hbm, act_hbm, out_hbm, picked_ref, basis_ref, act_ref, turned_ref, own_ref, sems):
    features, rank = basis_ref.shape
    tokens = act_ref.shape[0]
    half = rank // 2
    load_basis = pltpu.make_async_copy(basis_hbm, basis_ref, sems.at[0])
    load_act = pltpu.make_async_copy(act_hbm, act_ref, sems.at[1])
    load_basis.start()
    load_act.start()
    load_basis.wait()
    turned_ref[...] = basis_ref[...].T.reshape(turned_ref.shape)
    picked = turned_ref[:, pl.ds(core_ref[0], 1)].reshape(half, features)
    picked_ref[...] = picked
    load_act.wait()
    copies = project_rows(picked, act_ref, own_ref, out_hbm.at[:, pl.ds(0, tokens)], sems.at[pl.ds(2, 2)])
    for copy in copies:
        copy.wait()


def project_other(picked_ref, act_ref, _, out_hbm, other_ref, sems):
    tokens = act_ref.shape[0]
    copies = project_rows(picked_ref[...], act_ref, other_ref, out_hbm.at[:, pl.ds(tokens, tokens)], sems)
    for copy in copies:
        copy.wait()


def grad_terms(summed_ref, own_ref, other_hbm, pieces_ref, out_ref, other_ref, total_ref, sem):
    tokens = own_ref.shape[0]
    chips, rows, rank = pieces_ref.shape
    load = pltpu.make_async_copy(other_hbm, other_ref, sem)
    load.start()
    own_rows = total_ref.shape[0] // chips
    total_ref[...] = jnp.dot(summed_ref[:, :tokens], own_ref[...], preferred_element_type=jnp.float32)
    at = own_rows * (total_ref.shape[1] // LANES)
    for i in range(0, rank, LANES):
        out_ref[:, at : at + rows, :] = pieces_ref[:, :, i : i + LANES]
        at += rows
    load.wait()
    half = chips // 2
    for j in range(0, chips, half):
        these = slice(j * own_rows, (j + half) * own_rows)
        more = jnp.dot(summed_ref[these, tokens:], other_ref[...], preferred_element_type=jnp.float32)
        total = (total_ref[these, :] + more).astype(jnp.bfloat16)
        at = 0
        for i in range(0, total.shape[1], LANES):
            out_ref[j : j + half, at : at + own_rows, :] = total[:, i : i + LANES].reshape(half, own_rows, LANES)
            at += own_rows


def adam(terms_ref, first_ref, second_ref, moment_ref, square_ref, copies_ref):
    own_rows, columns = first_ref.shape
    size = own_rows * (columns // LANES)
    total = terms_ref[0, :size, :].astype(jnp.float32)
    for i in range(1, terms_ref.shape[0]):
        total += terms_ref[i, :size, :].astype(jnp.float32)
    gradient = jnp.concatenate([total[i : i + own_rows] for i in range(0, size, own_rows)], 1)
    moment_next = decay_first * first_ref[...] + (1.0 - decay_first) * gradient
    square_next = decay_second * second_ref[...] + (1.0 - decay_second) * gradient * gradient
    moment_ref[...] = moment_next
    square_ref[...] = square_next
    direction = (moment_next / (jnp.sqrt(square_next) + epsilon)).astype(jnp.bfloat16)
    for i in range(copies_ref.shape[0]):
        copies_ref[i] = direction


def expand_own(core_ref, terms_ref, mine_ref, out_ref, rest_ref, block_ref):
    rows, half = rest_ref.shape
    chips, own_rows, columns = mine_ref.shape
    piece = rows // chips
    at = own_rows * (columns // LANES)
    for i in range(0, 2 * half, LANES):
        block_ref[:, i : i + LANES] = terms_ref[:, at : at + piece, :].reshape(rows, LANES)
        at += piece

    def columns_of(side):
        at = lax.broadcasted_iota(jnp.int32, (half // 2, half), 0)
        wanted = at // own_rows * (2 * own_rows) + side * own_rows + at % own_rows
        pick = (lax.broadcasted_iota(jnp.int32, (half // 2, half), 1) == wanted).astype(jnp.bfloat16)
        parts = (block_ref[:, :half], block_ref[:, half:])
        picked = [lax.dot_general(part, pick, LAST, preferred_element_type=jnp.float32) for part in parts]
        return jnp.concatenate(picked, 1).astype(jnp.bfloat16)

    direction = mine_ref[...].reshape(half, columns)
    out_ref[...] = jnp.dot(columns_of(core_ref[0]), direction, preferred_element_type=jnp.float32)
    rest_ref[...] = columns_of(1 - core_ref[0])


def expand(own_ref, rest_ref, other_ref, out_ref):
    direction = other_ref[...].reshape(rest_ref.shape[1], other_ref.shape[2])
    more = jnp.dot(rest_ref[...], direction, preferred_element_type=jnp.float32)
    out_ref[...] = (own_ref[...] + more).astype(jnp.bfloat16)


def body(activations, cotangent, basis, first_moment, second_moment):
    chips = lax.axis_size("chip")
    features, rank = basis.shape
    tokens = activations.shape[0]
    half = rank // 2
    own_rows, columns = first_moment.shape
    core = lax.axis_index("core").astype(jnp.int32).reshape(1)
    chip = lax.axis_index("chip").astype(jnp.int32).reshape(1)
    f32, bf16 = jnp.float32, jnp.bfloat16

    piece = features // (2 * chips)
    pieces = pl.pallas_call(
        give_pieces,
        out_shape=pltpu.HBM((lax.axis_size("fsdp"), piece, rank), bf16),
        in_specs=[IN_SMEM, IN_SMEM, IN_HBM],
        out_specs=IN_HBM,
        scratch_shapes=[pltpu.SemaphoreType.DMA((lax.axis_size("fsdp"),))],
        compiler_params=params(60 * 1024 * 1024),
        cost_estimate=cost(0, 1 << 20),
    )(core, chip, basis)
    pieces = lax.all_to_all(pieces, "fsdp", 0, 0, tiled=True)

    other_act = lax.ppermute(activations, "core", SWAP)
    other_cot = lax.ppermute(cotangent, "core", SWAP)
    width = 2 * tokens
    partial, picked = pl.pallas_call(
        project_own,
        out_shape=(pltpu.HBM((half, width), f32), pltpu.VMEM((half, features), bf16)),
        in_specs=[IN_SMEM, IN_HBM, IN_HBM],
        out_specs=(IN_HBM, IN_VMEM),
        scratch_shapes=[
            pltpu.VMEM((features, rank), bf16),
            pltpu.VMEM((tokens, features), bf16),
            pltpu.VMEM((chips, 2, own_rows, features), bf16),
            pltpu.VMEM((half, tokens), f32),
            pltpu.SemaphoreType.DMA((4,)),
        ],
        compiler_params=params(60 * 1024 * 1024),
        cost_estimate=cost(2 * rank * tokens * features, 5 << 20),
    )(core, basis, activations)
    partial = pl.pallas_call(
        project_other,
        out_shape=pltpu.HBM((half, width), f32),
        in_specs=[IN_VMEM, IN_VMEM, IN_HBM],
        out_specs=IN_HBM,
        scratch_shapes=[pltpu.VMEM((half, tokens), f32), pltpu.SemaphoreType.DMA((2,))],
        input_output_aliases={2: 0},
        compiler_params=params(),
        cost_estimate=cost(rank * tokens * features, 3 << 20),
    )(picked, other_act, partial)
    summed = lax.psum(partial, "fsdp").astype(bf16)

    terms = pl.pallas_call(
        grad_terms,
        out_shape=jax.ShapeDtypeStruct((chips, (own_rows * columns + piece * rank) // LANES, LANES), bf16),
        in_specs=[IN_VMEM, IN_VMEM, IN_HBM, IN_VMEM],
        out_specs=IN_VMEM,
        scratch_shapes=[
            pltpu.VMEM((tokens, columns), bf16),
            pltpu.VMEM((half, columns), f32),
            pltpu.SemaphoreType.DMA,
        ],
        compiler_params=params(GRAD_LIMIT),
        cost_estimate=cost(2 * rank * tokens * columns, 5 << 20),
    )(summed, cotangent, other_cot, pieces)
    terms = lax.all_to_all(terms, "chip", 0, 0, tiled=True)

    moment_next, square_next, copies = pl.pallas_call(
        adam,
        out_shape=(
            jax.ShapeDtypeStruct((own_rows, columns), f32),
            jax.ShapeDtypeStruct((own_rows, columns), f32),
            jax.ShapeDtypeStruct((chips, own_rows, columns), bf16),
        ),
        in_specs=[IN_VMEM] * 3,
        out_specs=(IN_VMEM,) * 3,
        compiler_params=params(),
        cost_estimate=cost(1 << 20, 2 << 20),
    )(terms, first_moment, second_moment)
    mine = lax.all_to_all(copies, "chip", 0, 0, tiled=True)
    other = lax.ppermute(mine, "core", SWAP)
    rows = features // 2
    own, rest = pl.pallas_call(
        expand_own,
        out_shape=(pltpu.VMEM((rows, columns), f32), pltpu.VMEM((rows, half), bf16)),
        in_specs=[IN_SMEM, IN_VMEM, IN_VMEM],
        out_specs=(IN_VMEM, IN_VMEM),
        scratch_shapes=[pltpu.VMEM((rows, rank), bf16)],
        compiler_params=params(),
        cost_estimate=cost(rows * rank * columns, 3 << 20),
    )(core, terms, mine)
    expanded = pl.pallas_call(
        expand,
        out_shape=jax.ShapeDtypeStruct((rows, columns), bf16),
        in_specs=[IN_VMEM] * 3,
        out_specs=IN_VMEM,
        compiler_params=params(),
        cost_estimate=cost(rows * rank * columns, 3 << 20),
    )(own, rest, other)
    return (moment_next, square_next, expanded)


def solution(mesh):
    devices = np.asarray(mesh.devices)
    inner = Mesh(devices.reshape(devices.shape[0] // 2, 2, devices.shape[1]), ("chip", "core", "fsdp"))
    split = P(("chip", "core"), "fsdp")
    in_specs = (split, split, P("fsdp", None), split, split)
    return jax.shard_map(body, mesh=inner, in_specs=in_specs, out_specs=(split, split, split), check_vma=False)
```

```python
import numpy as np
import jax
import jax.numpy as jnp
from jax import lax
from jax.experimental import pallas as pl
from jax.experimental.pallas import tpu as pltpu
from jax.sharding import Mesh, PartitionSpec as P

decay_first = 0.9
decay_second = 0.999
epsilon = 1e-08

SWAP = [(0, 1), (1, 0)]
VMEM_LIMIT = 40 * 1024 * 1024
OWN_LIMIT = 60 * 1024 * 1024
LAST = (((1,), (1,)), ((), ()))
IN_VMEM = pl.BlockSpec(memory_space=pltpu.VMEM)
IN_HBM = pl.BlockSpec(memory_space=pltpu.HBM)
IN_SMEM = pl.BlockSpec(memory_space=pltpu.SMEM)


def params(limit=VMEM_LIMIT):
    return pltpu.CompilerParams(vmem_limit_bytes=limit)


def cost(flops, moved):
    return pl.CostEstimate(flops=flops, bytes_accessed=moved, transcendentals=0)


def project_own(core_ref, holds_ref, basis_hbm, act_hbm, own_ref, block_ref, picked_ref, basis_ref, act_ref, turned_ref, sems):
    features, rank = basis_ref.shape
    half = rank // 2
    rows = features // 2
    load_basis = pltpu.make_async_copy(basis_hbm, basis_ref, sems.at[0])
    load_act = pltpu.make_async_copy(act_hbm, act_ref, sems.at[1])
    load_basis.start()
    load_act.start()
    load_basis.wait()
    mine = basis_ref[pl.ds(pl.multiple_of(core_ref[0] * rows, rows), rows), :].astype(jnp.float32)
    mine = jnp.where(holds_ref[0] == 1, mine, 0.0)
    block_ref[:rows, :] = mine[:, :half]
    block_ref[rows:, :] = mine[:, half:]
    turned_ref[...] = basis_ref[...].T.reshape(turned_ref.shape)
    picked = turned_ref[:, pl.ds(core_ref[0], 1)].reshape(half, features)
    picked_ref[...] = picked
    load_act.wait()
    own_ref[...] = lax.dot_general(picked, act_ref[...], LAST, preferred_element_type=jnp.float32)


def project_other(picked_ref, act_ref, own_ref, block_ref, out_hbm, other_ref, sems):
    tokens = act_ref.shape[0]
    half = block_ref.shape[0]
    copies = [
        pltpu.make_async_copy(own_ref, out_hbm.at[:, pl.ds(0, tokens)], sems.at[0]),
        pltpu.make_async_copy(block_ref, out_hbm.at[:, pl.ds(2 * tokens, half)], sems.at[1]),
    ]
    for copy in copies:
        copy.start()
    part = half // 2
    for i in range(2):
        rows = pl.ds(i * part, part)
        other_ref[rows, :] = lax.dot_general(picked_ref[rows, :], act_ref[...], LAST, preferred_element_type=jnp.float32)
        copies.append(
            pltpu.make_async_copy(other_ref.at[rows, :], out_hbm.at[rows, pl.ds(tokens, tokens)], sems.at[2 + i])
        )
        copies[-1].start()
    for copy in copies:
        copy.wait()


def own_terms(summed_ref, own_ref, other_hbm, out_ref, other_ref, sem):
    tokens = own_ref.shape[0]
    load = pltpu.make_async_copy(other_hbm, other_ref, sem)
    load.start()
    out_ref[...] = jnp.dot(summed_ref[:, :tokens], own_ref[...], preferred_element_type=jnp.float32)
    load.wait()


def all_terms(own_ref, summed_ref, other_ref, out_ref):
    tokens = other_ref.shape[0]
    more = jnp.dot(summed_ref[:, tokens : 2 * tokens], other_ref[...], preferred_element_type=jnp.float32)
    out_ref[...] = (own_ref[...] + more).astype(jnp.bfloat16)


def adam(terms_ref, first_ref, second_ref, moment_ref, square_ref, copies_ref):
    gradient = terms_ref[0].astype(jnp.float32)
    for i in range(1, terms_ref.shape[0]):
        gradient += terms_ref[i].astype(jnp.float32)
    moment_next = decay_first * first_ref[...] + (1.0 - decay_first) * gradient
    square_next = decay_second * second_ref[...] + (1.0 - decay_second) * gradient * gradient
    moment_ref[...] = moment_next
    square_ref[...] = square_next
    direction = (moment_next / (jnp.sqrt(square_next) + epsilon)).astype(jnp.bfloat16)
    for i in range(copies_ref.shape[0]):
        copies_ref[i] = direction


def expand_own(core_ref, summed_ref, mine_ref, moment_ref, square_ref, out_ref, rest_ref, moment_hbm, square_hbm, sems):
    saves = [
        pltpu.make_async_copy(moment_ref, moment_hbm, sems.at[0]),
        pltpu.make_async_copy(square_ref, square_hbm, sems.at[1]),
    ]
    for save in saves:
        save.start()
    rows, half = rest_ref.shape
    own_rows = mine_ref.shape[1]
    start = summed_ref.shape[1] - half
    left, right = summed_ref[:rows, start:], summed_ref[rows:, start:]

    def columns_of(side):
        at = lax.broadcasted_iota(jnp.int32, (half // 2, half), 0)
        wanted = at // own_rows * (2 * own_rows) + side * own_rows + at % own_rows
        pick = (lax.broadcasted_iota(jnp.int32, (half // 2, half), 1) == wanted).astype(jnp.bfloat16)
        picked = [lax.dot_general(part, pick, LAST, preferred_element_type=jnp.float32) for part in (left, right)]
        return jnp.concatenate(picked, 1).astype(jnp.bfloat16)

    direction = mine_ref[...].reshape(half, mine_ref.shape[2])
    out_ref[...] = jnp.dot(columns_of(core_ref[0]), direction, preferred_element_type=jnp.float32)
    rest_ref[...] = columns_of(1 - core_ref[0])
    for save in saves:
        save.wait()


def expand(own_ref, rest_ref, other_ref, out_ref):
    direction = other_ref[...].reshape(rest_ref.shape[1], other_ref.shape[2])
    more = jnp.dot(rest_ref[...], direction, preferred_element_type=jnp.float32)
    out_ref[...] = (own_ref[...] + more).astype(jnp.bfloat16)


def body(activations, cotangent, basis, first_moment, second_moment):
    chips = lax.axis_size("chip")
    features, rank = basis.shape
    tokens = activations.shape[0]
    half = rank // 2
    own_rows, columns = first_moment.shape
    core = lax.axis_index("core").astype(jnp.int32).reshape(1)
    holds = (lax.axis_index("chip") == lax.axis_index("fsdp")).astype(jnp.int32).reshape(1)
    f32, bf16 = jnp.float32, jnp.bfloat16

    other_act = lax.ppermute(activations, "core", SWAP)
    other_cot = lax.ppermute(cotangent, "core", SWAP)
    width = 2 * tokens + half
    own, block, picked = pl.pallas_call(
        project_own,
        out_shape=(
            pltpu.VMEM((half, tokens), f32),
            pltpu.VMEM((half, half), f32),
            pltpu.VMEM((half, features), bf16),
        ),
        in_specs=[IN_SMEM, IN_SMEM, IN_HBM, IN_HBM],
        out_specs=(IN_VMEM,) * 3,
        scratch_shapes=[
            pltpu.VMEM((features, rank), bf16),
            pltpu.VMEM((tokens, features), bf16),
            pltpu.VMEM((chips, 2, own_rows, features), bf16),
            pltpu.SemaphoreType.DMA((2,)),
        ],
        compiler_params=params(OWN_LIMIT),
        cost_estimate=cost(2 * rank * tokens * features, 5 << 20),
    )(core, holds, basis, activations)
    partial = pl.pallas_call(
        project_other,
        out_shape=pltpu.HBM((half, width), f32),
        in_specs=[IN_VMEM] * 4,
        out_specs=IN_HBM,
        scratch_shapes=[pltpu.VMEM((half, tokens), f32), pltpu.SemaphoreType.DMA((4,))],
        compiler_params=params(),
        cost_estimate=cost(rank * tokens * features, 3 << 20),
    )(picked, other_act, own, block)
    summed = lax.psum(partial, "fsdp").astype(bf16)

    own, other = pl.pallas_call(
        own_terms,
        out_shape=(pltpu.VMEM((half, columns), f32), pltpu.VMEM((tokens, columns), bf16)),
        in_specs=[IN_VMEM, IN_VMEM, IN_HBM],
        out_specs=(IN_VMEM, IN_VMEM),
        scratch_shapes=[pltpu.SemaphoreType.DMA],
        compiler_params=params(),
        cost_estimate=cost(rank * tokens * columns, 4 << 20),
    )(summed, cotangent, other_cot)
    terms = pl.pallas_call(
        all_terms,
        out_shape=jax.ShapeDtypeStruct((half, columns), bf16),
        in_specs=[IN_VMEM] * 3,
        out_specs=IN_VMEM,
        compiler_params=params(),
        cost_estimate=cost(rank * tokens * columns, 4 << 20),
    )(own, summed, other)
    terms = lax.all_to_all(terms.reshape(chips, own_rows, columns), "chip", 0, 0, tiled=True)

    moment_next, square_next, copies = pl.pallas_call(
        adam,
        out_shape=(
            pltpu.VMEM((own_rows, columns), f32),
            pltpu.VMEM((own_rows, columns), f32),
            jax.ShapeDtypeStruct((chips, own_rows, columns), bf16),
        ),
        in_specs=[IN_VMEM] * 3,
        out_specs=(IN_VMEM,) * 3,
        compiler_params=params(),
        cost_estimate=cost(1 << 20, 2 << 20),
    )(terms, first_moment, second_moment)
    mine = lax.all_to_all(copies, "chip", 0, 0, tiled=True)
    other = lax.ppermute(mine, "core", SWAP)
    rows = features // 2
    own, rest, moment_next, square_next = pl.pallas_call(
        expand_own,
        out_shape=(
            pltpu.VMEM((rows, columns), f32),
            pltpu.VMEM((rows, half), bf16),
            pltpu.HBM((own_rows, columns), f32),
            pltpu.HBM((own_rows, columns), f32),
        ),
        in_specs=[IN_SMEM] + [IN_VMEM] * 4,
        out_specs=(IN_VMEM, IN_VMEM, IN_HBM, IN_HBM),
        scratch_shapes=[pltpu.SemaphoreType.DMA((2,))],
        compiler_params=params(),
        cost_estimate=cost(rows * rank * columns, 3 << 20),
    )(core, summed, mine, moment_next, square_next)
    expanded = pl.pallas_call(
        expand,
        out_shape=jax.ShapeDtypeStruct((rows, columns), bf16),
        in_specs=[IN_VMEM] * 3,
        out_specs=IN_VMEM,
        compiler_params=params(),
        cost_estimate=cost(rows * rank * columns, 3 << 20),
    )(own, rest, other)
    return (moment_next, square_next, expanded)


def solution(mesh):
    devices = np.asarray(mesh.devices)
    inner = Mesh(devices.reshape(devices.shape[0] // 2, 2, devices.shape[1]), ("chip", "core", "fsdp"))
    split = P(("chip", "core"), "fsdp")
    in_specs = (split, split, P("fsdp", None), split, split)
    return jax.shard_map(body, mesh=inner, in_specs=in_specs, out_specs=(split, split, split), check_vma=False)
```

```python
import numpy as np
import jax
import jax.numpy as jnp
from jax import lax
from jax.experimental import pallas as pl
from jax.experimental.pallas import tpu as pltpu
from jax.sharding import Mesh, PartitionSpec as P

decay_first = 0.9
decay_second = 0.999
epsilon = 1e-08

SWAP = [(0, 1), (1, 0)]
VMEM_LIMIT = 40 * 1024 * 1024
OWN_LIMIT = 60 * 1024 * 1024
LAST = (((1,), (1,)), ((), ()))
IN_VMEM = pl.BlockSpec(memory_space=pltpu.VMEM)
IN_HBM = pl.BlockSpec(memory_space=pltpu.HBM)
IN_SMEM = pl.BlockSpec(memory_space=pltpu.SMEM)


def params(limit=VMEM_LIMIT):
    return pltpu.CompilerParams(vmem_limit_bytes=limit)


def cost(flops, moved):
    return pl.CostEstimate(flops=flops, bytes_accessed=moved, transcendentals=0)


def project_own(core_ref, holds_ref, basis_hbm, act_hbm, out_hbm, own_ref, picked_ref, basis_ref, act_ref, turned_ref, block_ref, sems):
    tokens, features = act_ref.shape
    parts, _, wide = basis_ref.shape
    rows = features // 2
    groups = turned_ref.shape[0] // parts
    size = picked_ref.shape[0] // parts
    first = pl.multiple_of(core_ref[0] * rows, rows)
    loads = [pltpu.make_async_copy(basis_hbm.at[:, pl.ds(i * wide, wide)], basis_ref.at[i], sems.at[i]) for i in range(parts)]
    load_act = pltpu.make_async_copy(act_hbm, act_ref, sems.at[parts])
    loads[0].start()
    load_act.start()
    for load in loads[1:]:
        load.start()
    saves = []
    for i in range(parts):
        loads[i].wait()
        mine = basis_ref[i, pl.ds(first, rows), :].astype(jnp.float32)
        here = pl.ds(i * rows, rows)
        block_ref[here, :] = jnp.where(holds_ref[0] == 1, mine, 0.0)
        saves.append(
            pltpu.make_async_copy(block_ref.at[here, :], out_hbm.at[here, pl.ds(2 * tokens, wide)], sems.at[parts + 1 + i])
        )
        saves[i].start()
        these = pl.ds(i * groups, groups)
        turned_ref[these] = basis_ref[i].T.reshape(groups, *turned_ref.shape[1:])
        picked = turned_ref[these, pl.ds(core_ref[0], 1)].reshape(size, features)
        picked_ref[pl.ds(i * size, size), :] = picked
        if i == 0:
            load_act.wait()
        own_ref[pl.ds(i * size, size), :] = lax.dot_general(picked, act_ref[...], LAST, preferred_element_type=jnp.float32)
    for save in saves:
        save.wait()


def project_other(picked_ref, act_ref, own_ref, _, out_hbm, other_ref, sems):
    half, tokens = own_ref.shape
    copies = [pltpu.make_async_copy(own_ref, out_hbm.at[:, pl.ds(0, tokens)], sems.at[0])]
    copies[0].start()
    part = half // 2
    for i in range(2):
        rows = pl.ds(i * part, part)
        other_ref[rows, :] = lax.dot_general(picked_ref[rows, :], act_ref[...], LAST, preferred_element_type=jnp.float32)
        copies.append(
            pltpu.make_async_copy(other_ref.at[rows, :], out_hbm.at[rows, pl.ds(tokens, tokens)], sems.at[1 + i])
        )
        copies[-1].start()
    for copy in copies:
        copy.wait()


def own_terms(summed_ref, own_ref, other_hbm, out_ref, other_ref, sem):
    tokens = own_ref.shape[0]
    load = pltpu.make_async_copy(other_hbm, other_ref, sem)
    load.start()
    out_ref[...] = jnp.dot(summed_ref[:, :tokens], own_ref[...], preferred_element_type=jnp.float32)
    load.wait()


def all_terms(own_ref, summed_ref, other_ref, out_ref):
    tokens = other_ref.shape[0]
    more = jnp.dot(summed_ref[:, tokens : 2 * tokens], other_ref[...], preferred_element_type=jnp.float32)
    out_ref[...] = (own_ref[...] + more).astype(jnp.bfloat16)


def adam(terms_ref, first_ref, second_ref, moment_ref, square_ref, copies_ref):
    gradient = terms_ref[0].astype(jnp.float32)
    for i in range(1, terms_ref.shape[0]):
        gradient += terms_ref[i].astype(jnp.float32)
    moment_next = decay_first * first_ref[...] + (1.0 - decay_first) * gradient
    square_next = decay_second * second_ref[...] + (1.0 - decay_second) * gradient * gradient
    moment_ref[...] = moment_next
    square_ref[...] = square_next
    direction = (moment_next / (jnp.sqrt(square_next) + epsilon)).astype(jnp.bfloat16)
    for i in range(copies_ref.shape[0]):
        copies_ref[i] = direction


def expand_own(core_ref, summed_ref, mine_ref, moment_ref, square_ref, out_ref, rest_ref, moment_hbm, square_hbm, sems):
    saves = [
        pltpu.make_async_copy(moment_ref, moment_hbm, sems.at[0]),
        pltpu.make_async_copy(square_ref, square_hbm, sems.at[1]),
    ]
    for save in saves:
        save.start()
    rows, half = rest_ref.shape
    own_rows = mine_ref.shape[1]
    start = summed_ref.shape[1] - half
    left, right = summed_ref[:rows, start:], summed_ref[rows:, start:]

    def columns_of(side):
        at = lax.broadcasted_iota(jnp.int32, (half // 2, half), 0)
        wanted = at // own_rows * (2 * own_rows) + side * own_rows + at % own_rows
        pick = (lax.broadcasted_iota(jnp.int32, (half // 2, half), 1) == wanted).astype(jnp.bfloat16)
        picked = [lax.dot_general(part, pick, LAST, preferred_element_type=jnp.float32) for part in (left, right)]
        return jnp.concatenate(picked, 1).astype(jnp.bfloat16)

    direction = mine_ref[...].reshape(half, mine_ref.shape[2])
    out_ref[...] = jnp.dot(columns_of(core_ref[0]), direction, preferred_element_type=jnp.float32)
    rest_ref[...] = columns_of(1 - core_ref[0])
    for save in saves:
        save.wait()


def expand(own_ref, rest_ref, other_ref, out_hbm, out_ref, sems):
    direction = other_ref[...].reshape(rest_ref.shape[1], other_ref.shape[2])
    part = out_ref.shape[0] // 2
    saves = []
    for i in range(2):
        rows = pl.ds(i * part, part)
        more = jnp.dot(rest_ref[rows, :], direction, preferred_element_type=jnp.float32)
        out_ref[rows, :] = (own_ref[rows, :] + more).astype(jnp.bfloat16)
        saves.append(pltpu.make_async_copy(out_ref.at[rows, :], out_hbm.at[rows, :], sems.at[i]))
        saves[i].start()
    for save in saves:
        save.wait()


def body(activations, cotangent, basis, first_moment, second_moment):
    chips = lax.axis_size("chip")
    features, rank = basis.shape
    tokens = activations.shape[0]
    half = rank // 2
    own_rows, columns = first_moment.shape
    core = lax.axis_index("core").astype(jnp.int32).reshape(1)
    holds = (lax.axis_index("chip") == lax.axis_index("fsdp")).astype(jnp.int32).reshape(1)
    f32, bf16 = jnp.float32, jnp.bfloat16

    other_act = lax.ppermute(activations, "core", SWAP)
    other_cot = lax.ppermute(cotangent, "core", SWAP)
    width = 2 * tokens + half
    partial, own, picked = pl.pallas_call(
        project_own,
        out_shape=(
            pltpu.HBM((half, width), f32),
            pltpu.VMEM((half, tokens), f32),
            pltpu.VMEM((half, features), bf16),
        ),
        in_specs=[IN_SMEM, IN_SMEM, IN_HBM, IN_HBM],
        out_specs=(IN_HBM, IN_VMEM, IN_VMEM),
        scratch_shapes=[
            pltpu.VMEM((2, features, half), bf16),
            pltpu.VMEM((tokens, features), bf16),
            pltpu.VMEM((chips, 2, own_rows, features), bf16),
            pltpu.VMEM((features, half), f32),
            pltpu.SemaphoreType.DMA((5,)),
        ],
        compiler_params=params(OWN_LIMIT),
        cost_estimate=cost(2 * rank * tokens * features, 5 << 20),
    )(core, holds, basis, activations)
    partial = pl.pallas_call(
        project_other,
        out_shape=pltpu.HBM((half, width), f32),
        in_specs=[IN_VMEM] * 3 + [IN_HBM],
        out_specs=IN_HBM,
        scratch_shapes=[pltpu.VMEM((half, tokens), f32), pltpu.SemaphoreType.DMA((3,))],
        input_output_aliases={3: 0},
        compiler_params=params(),
        cost_estimate=cost(rank * tokens * features, 3 << 20),
    )(picked, other_act, own, partial)
    summed = lax.psum(partial, "fsdp").astype(bf16)

    own, other = pl.pallas_call(
        own_terms,
        out_shape=(pltpu.VMEM((half, columns), f32), pltpu.VMEM((tokens, columns), bf16)),
        in_specs=[IN_VMEM, IN_VMEM, IN_HBM],
        out_specs=(IN_VMEM, IN_VMEM),
        scratch_shapes=[pltpu.SemaphoreType.DMA],
        compiler_params=params(),
        cost_estimate=cost(rank * tokens * columns, 4 << 20),
    )(summed, cotangent, other_cot)
    terms = pl.pallas_call(
        all_terms,
        out_shape=jax.ShapeDtypeStruct((half, columns), bf16),
        in_specs=[IN_VMEM] * 3,
        out_specs=IN_VMEM,
        compiler_params=params(),
        cost_estimate=cost(rank * tokens * columns, 4 << 20),
    )(own, summed, other)
    terms = lax.all_to_all(terms.reshape(chips, own_rows, columns), "chip", 0, 0, tiled=True)

    moment_next, square_next, copies = pl.pallas_call(
        adam,
        out_shape=(
            pltpu.VMEM((own_rows, columns), f32),
            pltpu.VMEM((own_rows, columns), f32),
            jax.ShapeDtypeStruct((chips, own_rows, columns), bf16),
        ),
        in_specs=[IN_VMEM] * 3,
        out_specs=(IN_VMEM,) * 3,
        compiler_params=params(),
        cost_estimate=cost(1 << 20, 2 << 20),
    )(terms, first_moment, second_moment)
    mine = lax.all_to_all(copies, "chip", 0, 0, tiled=True)
    other = lax.ppermute(mine, "core", SWAP)
    rows = features // 2
    own, rest, moment_next, square_next = pl.pallas_call(
        expand_own,
        out_shape=(
            pltpu.VMEM((rows, columns), f32),
            pltpu.VMEM((rows, half), bf16),
            pltpu.HBM((own_rows, columns), f32),
            pltpu.HBM((own_rows, columns), f32),
        ),
        in_specs=[IN_SMEM] + [IN_VMEM] * 4,
        out_specs=(IN_VMEM, IN_VMEM, IN_HBM, IN_HBM),
        scratch_shapes=[pltpu.SemaphoreType.DMA((2,))],
        compiler_params=params(),
        cost_estimate=cost(rows * rank * columns, 3 << 20),
    )(core, summed, mine, moment_next, square_next)
    expanded = pl.pallas_call(
        expand,
        out_shape=pltpu.HBM((rows, columns), bf16),
        in_specs=[IN_VMEM] * 3,
        out_specs=IN_HBM,
        scratch_shapes=[pltpu.VMEM((rows, columns), bf16), pltpu.SemaphoreType.DMA((2,))],
        compiler_params=params(),
        cost_estimate=cost(rows * rank * columns, 3 << 20),
    )(own, rest, other)
    return (moment_next, square_next, expanded)


def solution(mesh):
    devices = np.asarray(mesh.devices)
    inner = Mesh(devices.reshape(devices.shape[0] // 2, 2, devices.shape[1]), ("chip", "core", "fsdp"))
    split = P(("chip", "core"), "fsdp")
    in_specs = (split, split, P("fsdp", None), split, split)
    return jax.shard_map(body, mesh=inner, in_specs=in_specs, out_specs=(split, split, split), check_vma=False)
```

```python
import numpy as np
import jax
import jax.numpy as jnp
from jax import lax
from jax.experimental import pallas as pl
from jax.experimental.pallas import tpu as pltpu
from jax.sharding import Mesh, PartitionSpec as P

decay_first = 0.9
decay_second = 0.999
epsilon = 1e-08

SWAP = [(0, 1), (1, 0)]
VMEM_LIMIT = 40 * 1024 * 1024
OWN_LIMIT = 60 * 1024 * 1024
LAST = (((1,), (1,)), ((), ()))
IN_VMEM = pl.BlockSpec(memory_space=pltpu.VMEM)
IN_HBM = pl.BlockSpec(memory_space=pltpu.HBM)
IN_SMEM = pl.BlockSpec(memory_space=pltpu.SMEM)


def params(limit=VMEM_LIMIT):
    return pltpu.CompilerParams(vmem_limit_bytes=limit)


def cost(flops, moved):
    return pl.CostEstimate(flops=flops, bytes_accessed=moved, transcendentals=0)


def project_own(core_ref, holds_ref, basis_hbm, act_hbm, out_hbm, own_ref, picked_ref, basis_ref, act_ref, turned_ref, block_ref, sems):
    features, rank = basis_ref.shape
    half = rank // 2
    rows = features // 2
    load_basis = pltpu.make_async_copy(basis_hbm, basis_ref, sems.at[0])
    load_act = pltpu.make_async_copy(act_hbm, act_ref, sems.at[1])
    load_basis.start()
    load_act.start()
    load_basis.wait()
    mine = basis_ref[pl.ds(pl.multiple_of(core_ref[0] * rows, rows), rows), :].astype(jnp.float32)
    mine = jnp.where(holds_ref[0] == 1, mine, 0.0)
    block_ref[:rows, :] = mine[:, :half]
    block_ref[rows:, :] = mine[:, half:]
    save = pltpu.make_async_copy(block_ref, out_hbm.at[:, pl.ds(2 * act_ref.shape[0], half)], sems.at[2])
    save.start()
    turned_ref[...] = basis_ref[...].T.reshape(turned_ref.shape)
    picked = turned_ref[:, pl.ds(core_ref[0], 1)].reshape(half, features)
    picked_ref[...] = picked
    load_act.wait()
    own_ref[...] = lax.dot_general(picked, act_ref[...], LAST, preferred_element_type=jnp.float32)
    save.wait()


def project_other(picked_ref, act_ref, own_ref, _, out_hbm, other_ref, sems):
    half, tokens = own_ref.shape
    copies = [pltpu.make_async_copy(own_ref, out_hbm.at[:, pl.ds(0, tokens)], sems.at[0])]
    copies[0].start()
    part = half // 2
    for i in range(2):
        rows = pl.ds(i * part, part)
        other_ref[rows, :] = lax.dot_general(picked_ref[rows, :], act_ref[...], LAST, preferred_element_type=jnp.float32)
        copies.append(
            pltpu.make_async_copy(other_ref.at[rows, :], out_hbm.at[rows, pl.ds(tokens, tokens)], sems.at[1 + i])
        )
        copies[-1].start()
    for copy in copies:
        copy.wait()


def own_terms(summed_ref, own_ref, other_hbm, out_ref, other_ref, sem):
    tokens = own_ref.shape[0]
    load = pltpu.make_async_copy(other_hbm, other_ref, sem)
    load.start()
    out_ref[...] = jnp.dot(summed_ref[:, :tokens], own_ref[...], preferred_element_type=jnp.float32)
    load.wait()


def all_terms(own_ref, summed_ref, other_ref, out_ref):
    tokens = other_ref.shape[0]
    more = jnp.dot(summed_ref[:, tokens : 2 * tokens], other_ref[...], preferred_element_type=jnp.float32)
    out_ref[...] = (own_ref[...] + more).astype(jnp.bfloat16)


def adam(terms_ref, first_ref, second_ref, moment_ref, square_ref, copies_ref):
    gradient = terms_ref[0].astype(jnp.float32)
    for i in range(1, terms_ref.shape[0]):
        gradient += terms_ref[i].astype(jnp.float32)
    moment_next = decay_first * first_ref[...] + (1.0 - decay_first) * gradient
    square_next = decay_second * second_ref[...] + (1.0 - decay_second) * gradient * gradient
    moment_ref[...] = moment_next
    square_ref[...] = square_next
    direction = (moment_next / (jnp.sqrt(square_next) + epsilon)).astype(jnp.bfloat16)
    for i in range(copies_ref.shape[0]):
        copies_ref[i] = direction


def expand_own(core_ref, summed_ref, mine_ref, moment_ref, square_ref, out_ref, rest_ref, moment_hbm, square_hbm, sems):
    saves = [
        pltpu.make_async_copy(moment_ref, moment_hbm, sems.at[0]),
        pltpu.make_async_copy(square_ref, square_hbm, sems.at[1]),
    ]
    for save in saves:
        save.start()
    rows, half = rest_ref.shape
    own_rows = mine_ref.shape[1]
    start = summed_ref.shape[1] - half
    left, right = summed_ref[:rows, start:], summed_ref[rows:, start:]

    def columns_of(side):
        at = lax.broadcasted_iota(jnp.int32, (half // 2, half), 0)
        wanted = at // own_rows * (2 * own_rows) + side * own_rows + at % own_rows
        pick = (lax.broadcasted_iota(jnp.int32, (half // 2, half), 1) == wanted).astype(jnp.bfloat16)
        picked = [lax.dot_general(part, pick, LAST, preferred_element_type=jnp.float32) for part in (left, right)]
        return jnp.concatenate(picked, 1).astype(jnp.bfloat16)

    direction = mine_ref[...].reshape(half, mine_ref.shape[2])
    out_ref[...] = jnp.dot(columns_of(core_ref[0]), direction, preferred_element_type=jnp.float32)
    rest_ref[...] = columns_of(1 - core_ref[0])
    for save in saves:
        save.wait()


def expand(own_ref, rest_ref, other_ref, out_hbm, out_ref, sems):
    direction = other_ref[...].reshape(rest_ref.shape[1], other_ref.shape[2])
    part = out_ref.shape[0] // 2
    saves = []
    for i in range(2):
        rows = pl.ds(i * part, part)
        more = jnp.dot(rest_ref[rows, :], direction, preferred_element_type=jnp.float32)
        out_ref[rows, :] = (own_ref[rows, :] + more).astype(jnp.bfloat16)
        saves.append(pltpu.make_async_copy(out_ref.at[rows, :], out_hbm.at[rows, :], sems.at[i]))
        saves[i].start()
    for save in saves:
        save.wait()


def body(activations, cotangent, basis, first_moment, second_moment):
    chips = lax.axis_size("chip")
    features, rank = basis.shape
    tokens = activations.shape[0]
    half = rank // 2
    own_rows, columns = first_moment.shape
    core = lax.axis_index("core").astype(jnp.int32).reshape(1)
    holds = (lax.axis_index("chip") == lax.axis_index("fsdp")).astype(jnp.int32).reshape(1)
    f32, bf16 = jnp.float32, jnp.bfloat16

    other_act = lax.ppermute(activations, "core", SWAP)
    other_cot = lax.ppermute(cotangent, "core", SWAP)
    width = 2 * tokens + half
    partial, own, picked = pl.pallas_call(
        project_own,
        out_shape=(
            pltpu.HBM((half, width), f32),
            pltpu.VMEM((half, tokens), f32),
            pltpu.VMEM((half, features), bf16),
        ),
        in_specs=[IN_SMEM, IN_SMEM, IN_HBM, IN_HBM],
        out_specs=(IN_HBM, IN_VMEM, IN_VMEM),
        scratch_shapes=[
            pltpu.VMEM((features, rank), bf16),
            pltpu.VMEM((tokens, features), bf16),
            pltpu.VMEM((chips, 2, own_rows, features), bf16),
            pltpu.VMEM((half, half), f32),
            pltpu.SemaphoreType.DMA((3,)),
        ],
        compiler_params=params(OWN_LIMIT),
        cost_estimate=cost(2 * rank * tokens * features, 5 << 20),
    )(core, holds, basis, activations)
    partial = pl.pallas_call(
        project_other,
        out_shape=pltpu.HBM((half, width), f32),
        in_specs=[IN_VMEM] * 3 + [IN_HBM],
        out_specs=IN_HBM,
        scratch_shapes=[pltpu.VMEM((half, tokens), f32), pltpu.SemaphoreType.DMA((3,))],
        input_output_aliases={3: 0},
        compiler_params=params(),
        cost_estimate=cost(rank * tokens * features, 3 << 20),
    )(picked, other_act, own, partial)
    summed = lax.psum(partial, "fsdp").astype(bf16)

    own, other = pl.pallas_call(
        own_terms,
        out_shape=(pltpu.VMEM((half, columns), f32), pltpu.VMEM((tokens, columns), bf16)),
        in_specs=[IN_VMEM, IN_VMEM, IN_HBM],
        out_specs=(IN_VMEM, IN_VMEM),
        scratch_shapes=[pltpu.SemaphoreType.DMA],
        compiler_params=params(),
        cost_estimate=cost(rank * tokens * columns, 4 << 20),
    )(summed, cotangent, other_cot)
    terms = pl.pallas_call(
        all_terms,
        out_shape=jax.ShapeDtypeStruct((half, columns), bf16),
        in_specs=[IN_VMEM] * 3,
        out_specs=IN_VMEM,
        compiler_params=params(),
        cost_estimate=cost(rank * tokens * columns, 4 << 20),
    )(own, summed, other)
    terms = lax.all_to_all(terms.reshape(chips, own_rows, columns), "chip", 0, 0, tiled=True)

    moment_next, square_next, copies = pl.pallas_call(
        adam,
        out_shape=(
            pltpu.VMEM((own_rows, columns), f32),
            pltpu.VMEM((own_rows, columns), f32),
            jax.ShapeDtypeStruct((chips, own_rows, columns), bf16),
        ),
        in_specs=[IN_VMEM] * 3,
        out_specs=(IN_VMEM,) * 3,
        compiler_params=params(),
        cost_estimate=cost(1 << 20, 2 << 20),
    )(terms, first_moment, second_moment)
    mine = lax.all_to_all(copies, "chip", 0, 0, tiled=True)
    other = lax.ppermute(mine, "core", SWAP)
    rows = features // 2
    own, rest, moment_next, square_next = pl.pallas_call(
        expand_own,
        out_shape=(
            pltpu.VMEM((rows, columns), f32),
            pltpu.VMEM((rows, half), bf16),
            pltpu.HBM((own_rows, columns), f32),
            pltpu.HBM((own_rows, columns), f32),
        ),
        in_specs=[IN_SMEM] + [IN_VMEM] * 4,
        out_specs=(IN_VMEM, IN_VMEM, IN_HBM, IN_HBM),
        scratch_shapes=[pltpu.SemaphoreType.DMA((2,))],
        compiler_params=params(),
        cost_estimate=cost(rows * rank * columns, 3 << 20),
    )(core, summed, mine, moment_next, square_next)
    expanded = pl.pallas_call(
        expand,
        out_shape=pltpu.HBM((rows, columns), bf16),
        in_specs=[IN_VMEM] * 3,
        out_specs=IN_HBM,
        scratch_shapes=[pltpu.VMEM((rows, columns), bf16), pltpu.SemaphoreType.DMA((2,))],
        compiler_params=params(),
        cost_estimate=cost(rows * rank * columns, 3 << 20),
    )(own, rest, other)
    return (moment_next, square_next, expanded)


def solution(mesh):
    devices = np.asarray(mesh.devices)
    inner = Mesh(devices.reshape(devices.shape[0] // 2, 2, devices.shape[1]), ("chip", "core", "fsdp"))
    split = P(("chip", "core"), "fsdp")
    in_specs = (split, split, P("fsdp", None), split, split)
    return jax.shard_map(body, mesh=inner, in_specs=in_specs, out_specs=(split, split, split), check_vma=False)
```
